512 devices in a mesh: lat: 32 (over z_hi, y, core), chan: 4 (over z_lo), tm: 4 (over x).
Axes of the slice: x: 4, y: 8, z: 8 (z_hi: 2, z_lo: 4; z = z_hi * 4 + z_lo), core: 2. Of those that a mesh axis runs over, the one named last changes fastest.
Arguments:
- fields: bfloat16 [512, 1440, 256], P(('tm', 'lat'), None, 'chan'), parts along dimension 0, may hold values from -6 to 6
- disco_weight: bfloat16 [6, 256, 64], P(None, 'chan'), may hold values from -0.25 to 0.25
- support_lat: int32 [128, 9], P('lat'), may hold values from -2 to 2
- support_lon: int32 [128, 9], P('lat'), may hold values from -4 to 4
- support_basis: int32 [128, 9], P('lat'), may hold values from 0 to 5
- support_value: float32 [128, 9], P('lat'), may hold values from 0.25 to 1.5
- w_up: bfloat16 [256, 512], replicated, may hold values from -0.375 to 0.375
- w_down: bfloat16 [512, 256], replicated, may hold values from -0.25 to 0.25
- legendre: bfloat16 [384, 384, 128], P(('lat', 'chan')), may hold values from -0.5 to 0.5
Outputs:
- coefficients: bfloat16 [1536, 384, 512], P(('tm', 'lat', 'chan')), parts along dimension 0
The draws below stay inside these ranges and needn't reach their ends.
There are 4 independent parts, one for each index of `tm`. The reference program is written for one: setup_inputs(seed, part) draws one part's arguments, and reference() takes and returns one part's arrays. A program takes and returns all parts, laid end to end along the dimension named above; an argument that names none is the same for every part. Nothing has to cross between parts.
All inputs are finite; a program needn't handle non-finite values.
Results may differ from the reference program's by a relative error of at most 0.0076.
Values may be sent and summed in bfloat16 or wider, within the bound.
A program may use at most 128 MiB of HBM per device.

```python
import math
import jax
import jax.numpy as jnp
from jax import lax

C = 256
HID = 512
NLON = 1440
G = 64
NB = 6
S = 9
HALO = 2
DLON = 4
LL = 384
NLAT = 128
MM = 384


def set_ends(entries, own_key, low, high):
    extent = entries.shape
    place = [jax.random.randint(jax.random.fold_in(own_key, axis), (), 0, extent[axis]) for axis in range(len(extent))]
    entries = entries.at[tuple(place)].set(low)
    longest = extent.index(max(extent))
    place[longest] = (place[longest] + 1) % extent[longest]
    return entries.at[tuple(place)].set(high)


def levels(own_key, extent, pieces, smallest, largest):
    factor_of, own = 1.0, jax.random.fold_in(own_key, 6)
    for dim, parts in pieces:
        heights = jnp.exp(jax.random.uniform(jax.random.fold_in(own, dim), (parts,), jnp.float32, smallest / len(pieces), largest / len(pieces)))
        factor_of = factor_of * jnp.repeat(heights, extent[dim] // parts).reshape([-1 if axis == dim else 1 for axis in range(len(extent))])
    return factor_of


def scatter_about(key, extent, scale, most, shards=(), kind=jnp.bfloat16):
    values = jax.random.normal(key, extent, jnp.float32) * scale
    if len(shards) > 0:
        values = levels(key, extent, shards, -0.22, 0.18) * values
    return jnp.clip(values, min=-most, max=most).astype(kind)


def setup_inputs(seed: int = 0, part: int = 0) -> dict:
    splits = jax.random.split(jax.random.key(seed), 10)
    own_keys = jax.random.split(jax.random.fold_in(splits[9], part), 10)
    fields = scatter_about(own_keys[0], (NLAT, NLON, C), 1.0, 6.0, ((0, 32), (2, 4)))
    disco_weight = scatter_about(splits[1], (NB, C, G), (S * G) ** -0.5, 0.25, ((1, 4),))
    support_lat = set_ends(jax.random.randint(splits[2], (NLAT, S), 0 - HALO, HALO + 1), jax.random.fold_in(splits[2], 1), 0 - HALO, HALO).astype(jnp.int32)
    support_lon = set_ends(jax.random.randint(splits[3], (NLAT, S), 0 - DLON, DLON + 1), jax.random.fold_in(splits[3], 1), 0 - DLON, DLON).astype(jnp.int32)
    support_basis = set_ends(jax.random.randint(splits[4], (NLAT, S), 0, NB), jax.random.fold_in(splits[4], 1), 0, NB - 1).astype(jnp.int32)
    support_value = jnp.clip(0.25 + 1.25 * jax.random.uniform(splits[5], (NLAT, S), jnp.float32) ** levels(splits[5], (NLAT, S), ((0, 32),), -0.2, 0.2), 0.25, 1.5)
    w_up = scatter_about(splits[6], (C, HID), C ** -0.5, 0.375)
    w_down = scatter_about(splits[7], (HID, C), HID ** -0.5, 0.25)
    legendre = scatter_about(splits[8], (MM, LL, NLAT), NLAT ** -0.5, 0.5, ((0, 128),))
    return {"fields": fields, "disco_weight": disco_weight, "support_lat": support_lat, "support_lon": support_lon, "support_basis": support_basis, "support_value": support_value, "w_up": w_up, "w_down": w_down, "legendre": legendre}


def fourier_table(lon_count, mode_count):
    lon_index = jnp.arange(lon_count, dtype=jnp.int32)
    mode_index = jnp.arange(mode_count, dtype=jnp.int32)
    phase = lon_index[:, None] * mode_index[None, :] % lon_count
    angle = phase.astype(jnp.float32) * (2.0 * math.pi / lon_count)
    paired = jnp.stack([jnp.cos(angle), -jnp.sin(angle)], axis=-1) * math.sqrt(2.0 / lon_count)
    return paired.reshape(lon_count, 2 * mode_count).astype(jnp.bfloat16)

def channel_mlp(mixed, w_up, w_down):
    values = mixed.astype(jnp.float32)
    center = values - lax.optimization_barrier(jnp.mean(values, axis=-1, keepdims=True))
    spread = lax.optimization_barrier(jnp.mean(center * center, axis=-1, keepdims=True))
    normed = (center * lax.rsqrt(spread + 1e-05)).astype(jnp.bfloat16)
    lifted = jnp.einsum('anc,ch->anh', normed.astype(jnp.float32), w_up.astype(jnp.float32))
    active = jax.nn.gelu(lifted).astype(jnp.bfloat16)
    lowered = jnp.einsum('anh,hc->anc', active.astype(jnp.float32), w_down.astype(jnp.float32))
    return (values + lowered).astype(jnp.bfloat16)

def reference(fields, disco_weight, support_lat, support_lon, support_basis, support_value, w_up, w_down, legendre):
    lat_count, lon_count, chan_count = fields.shape
    group_count = chan_count // G
    padded = jnp.pad(fields, ((HALO, HALO), (0, 0), (0, 0)))
    row_ids = jnp.arange(lat_count, dtype=jnp.int32)
    lon_index = jnp.arange(lon_count, dtype=jnp.int32)
    weight_full = disco_weight.astype(jnp.float32)
    accumulated = jnp.zeros((lat_count, lon_count, group_count, G), jnp.float32)
    for position in range(S):
        source = (row_ids + HALO + support_lat[:, position]).astype(jnp.int32)
        columns = ((lon_index[None, :] + support_lon[:, position][:, None]) % lon_count).astype(jnp.int32)
        shifted = padded[source[:, None], columns].astype(jnp.float32).reshape(lat_count, lon_count, group_count, G)
        picked = weight_full[support_basis[:, position]] * support_value[:, position][:, None, None]
        rounded = lax.optimization_barrier(picked.astype(jnp.bfloat16))
        filters = rounded.astype(jnp.float32).reshape(lat_count, group_count, G, G)
        accumulated = accumulated + jnp.einsum('anhi,ahoi->anho', shifted, filters)
    mixed = (fields.astype(jnp.float32) + accumulated.reshape(lat_count, lon_count, chan_count)).astype(jnp.bfloat16)
    field_out = channel_mlp(mixed, w_up, w_down)
    fourier = fourier_table(lon_count, MM)
    spectrum = jnp.einsum('anc,nk->akc', field_out.astype(jnp.float32), fourier.astype(jnp.float32))
    spectrum = spectrum.astype(jnp.bfloat16).reshape(lat_count, MM, 2, chan_count)
    degree = jnp.arange(LL, dtype=jnp.int32)
    mode_ids = jnp.arange(MM, dtype=jnp.int32)
    kept_mask = degree[None, :] >= mode_ids[:, None]
    kept = jnp.where(kept_mask[:, :, None], legendre, jnp.zeros((), jnp.bfloat16))
    coefficients = jnp.einsum('mla,amrc->mlrc', kept.astype(jnp.float32), spectrum.astype(jnp.float32))
    return coefficients.reshape(MM, LL, 2 * chan_count).astype(jnp.bfloat16)
```

```python
import functools
import math

import jax
import jax.numpy as jnp
import ml_dtypes
import numpy as np
from jax import lax
from jax.experimental import pallas as pl
from jax.experimental.pallas import tpu as pltpu
from jax.sharding import PartitionSpec as P

G = 64
NB = 6
S = 9
HALO = 2
DLON = 4
LANES = 128
CHUNK = 384
PAD = 16


def fourier_rows(lon_count, lon_pad, mode_count, mode_dev):
    lon = np.arange(lon_count, dtype=np.int64)
    mode = np.arange(mode_count, dtype=np.int64)
    phase = (lon[:, None] * mode[None, :]) % lon_count
    angle = phase.astype(np.float32) * np.float32(2.0 * math.pi / lon_count)
    scale = np.float32(math.sqrt(2.0 / lon_count))
    table = np.zeros((mode_count // mode_dev, PAD // 2, lon_pad), np.float32)
    pair = np.stack([np.cos(angle), -np.sin(angle)], axis=-1) * scale
    pair = pair.reshape(lon_count, mode_count // mode_dev, 2 * mode_dev)
    table[:, : 2 * mode_dev, :lon_count] = np.transpose(pair, (1, 2, 0))
    return table.reshape(-1, lon_pad).astype(ml_dtypes.bfloat16)


def spread(block, ext, row, lon_count):
    chans = block.shape[0]
    tiles = -(-lon_count // LANES)
    last = lon_count - (tiles - 1) * LANES
    lane = lax.broadcasted_iota(jnp.int32, (chans, LANES), 1)
    pieces = [block[:, t * LANES : min((t + 1) * LANES, lon_count)].astype(jnp.float32) for t in range(tiles)]
    if last < LANES:
        pieces[-1] = jnp.concatenate([pieces[-1], jnp.zeros((chans, LANES - last), jnp.float32)], axis=1)
    turned = [pltpu.roll(p, DLON, 1) for p in pieces]
    before = pltpu.roll(pieces[-1], (LANES - last + DLON) % LANES, 1)
    after = pltpu.roll(pieces[0], last + DLON, 1)
    for t in range(tiles):
        left = before if t == 0 else turned[t - 1]
        value = jnp.where(lane < DLON, left, turned[t])
        if t == tiles - 1:
            value = jnp.where(lane < last + DLON, value, jnp.where(lane < last + 2 * DLON, after, 0.0))
        ext[row, :, t * LANES : (t + 1) * LANES] = value.astype(ext.dtype)
    ext[row, :, tiles * LANES :] = jnp.zeros((chans, ext.shape[2] - tiles * LANES), ext.dtype)


def make_filters(row, basis, value, twice, filters):
    lane = lax.broadcasted_iota(jnp.int32, (G, LANES), 1)
    for pair in range(0, S, 2):
        first = twice[basis[row, pair]].astype(jnp.float32) * value[row, pair]
        if pair + 1 < S:
            second = twice[basis[row, pair + 1]].astype(jnp.float32) * value[row, pair + 1]
            first = jnp.where(lane < G, first, second)
            filters[row, :, pair * G : (pair + 2) * G] = first.astype(filters.dtype)
        else:
            filters[row, :, pair * G : (pair + 1) * G] = first[:, :G].astype(filters.dtype)


def disco_chunk(row, start, shift_lat, shift_lon, ext, filters, columns):
    lane = lax.broadcasted_iota(jnp.int32, (G, LANES), 1)
    for tap in range(S):
        source = row + HALO + shift_lat[row, tap]
        turn = DLON + shift_lon[row, tap]
        held = ext[source, :, pl.ds(start, CHUNK + LANES)]
        turned = [
            pltpu.roll(held[:, t * LANES : (t + 1) * LANES], LANES - turn, 1)
            for t in range(CHUNK // LANES + 1)
        ]
        for t in range(CHUNK // LANES):
            columns[tap * G : (tap + 1) * G, t * LANES : (t + 1) * LANES] = jnp.where(
                lane < LANES - turn, turned[t], turned[t + 1]
            ).astype(columns.dtype)
    return jnp.dot(filters[row], columns[...], preferred_element_type=jnp.float32)


def disco_kernel(shift_lat, shift_lon, basis, value, fields, low, high, twice, out, ext, filters, columns):
    lat_dev, chans, lon_count = fields.shape
    chunks = out.shape[1]
    for r in range(HALO):
        spread(low[r], ext, r, lon_count)
        spread(high[r], ext, HALO + lat_dev + r, lon_count)
    for r in range(lat_dev):
        spread(fields[r], ext, HALO + r, lon_count)
        make_filters(r, basis, value, twice, filters)
    for c in range(chunks):
        start = c * CHUNK
        width = min(CHUNK, lon_count - start)
        for r in range(lat_dev):
            total = disco_chunk(r, start, shift_lat, shift_lon, ext, filters, columns)
            own = fields[r, :, start : start + width].astype(jnp.float32)
            out[r, c, :, :width] = (own + total[:, :width]).astype(out.dtype)
            if width < CHUNK:
                out[r, c, :, width:] = jnp.zeros((chans, CHUNK - width), out.dtype)


def mlp_chunk(mixed, up, down):
    values = mixed.astype(jnp.float32)
    center = values - jnp.mean(values, axis=0, keepdims=True)
    variance = jnp.mean(center * center, axis=0, keepdims=True)
    normed = (center * lax.rsqrt(variance + 1e-05)).astype(jnp.bfloat16)
    lifted = jnp.dot(up, normed, preferred_element_type=jnp.float32)
    inner = math.sqrt(2.0 / math.pi) * (lifted + 0.044715 * (lifted * lifted * lifted))
    active = (0.5 * lifted * (1.0 + jnp.tanh(inner))).astype(jnp.bfloat16)
    lowered = jnp.dot(down, active, preferred_element_type=jnp.float32)
    return (values + lowered).astype(jnp.bfloat16)


def store_spectrum(spectrum, out):
    half = PAD // 2
    for h in range(2):
        piece = spectrum[:, h * LANES : (h + 1) * LANES].astype(jnp.bfloat16)
        out[:, h * half : (h + 1) * half, :] = piece.reshape(out.shape[0], half, LANES)


def mlp_kernel(mixed, w_up, w_down, table, out):
    peers, chunks, chans, _ = mixed.shape
    up = w_up[...].T
    down = w_down[...].T
    total = None
    for c in range(chunks):
        block = jnp.concatenate([mixed[p, c] for p in range(peers)], axis=0)
        done = mlp_chunk(block, up, down)
        part = lax.dot_general(
            table[:, c * CHUNK : (c + 1) * CHUNK], done, (((1,), (1,)), ((), ())),
            preferred_element_type=jnp.float32,
        )
        total = part if total is None else total + part
    store_spectrum(total, out)


def legendre_kernel(spectrum, legendre, out, wide):
    lats = spectrum.shape[0]
    mode_dev, degrees, _ = legendre.shape
    me = lax.axis_index("lat") * lax.axis_size("chan") + lax.axis_index("chan")
    wide[...] = spectrum[...].astype(jnp.float32).reshape(lats * PAD, LANES)
    degree = lax.broadcasted_iota(jnp.int32, (degrees, lats), 0)
    for m in range(mode_dev):
        kept = jnp.where(degree >= me * mode_dev + m, legendre[m].astype(jnp.float32), 0.0).astype(jnp.bfloat16)
        rows = [h * (PAD // 2) + 2 * m + r for r in range(2) for h in range(2)]
        right = jnp.concatenate(
            [wide[pl.ds(j, lats, stride=PAD), :].astype(jnp.bfloat16) for j in rows], axis=1
        )
        out[m] = jnp.dot(kept, right, preferred_element_type=jnp.float32).astype(out.dtype)


def on_device(
    fields, disco_weight, support_lat, support_lon, support_basis, support_value, w_up, w_down, legendre
):
    lat_dev, lon_count, chans = fields.shape
    num_lat = lax.axis_size("lat")
    num_chan = lax.axis_size("chan")
    mode_dev, degrees, _ = legendre.shape
    devices = num_lat * num_chan
    chunks = -(-lon_count // CHUNK)
    smem = pl.BlockSpec(memory_space=pltpu.SMEM)
    vmem = pl.BlockSpec(memory_space=pltpu.VMEM)
    params = pltpu.CompilerParams(vmem_limit_bytes=56 << 20)
    turned = jnp.swapaxes(fields, 1, 2)
    twice = jnp.concatenate([disco_weight, disco_weight], axis=2)
    ends = num_lat - 1
    low = lax.ppermute(turned[lat_dev - HALO :], "lat", [(i, i + 1) for i in range(ends)])
    high = lax.ppermute(turned[:HALO], "lat", [(i + 1, i) for i in range(ends)])
    ext_lanes = chunks * CHUNK + LANES
    mixed = pl.pallas_call(
        disco_kernel,
        out_shape=jax.ShapeDtypeStruct((lat_dev, chunks, chans, CHUNK), jnp.bfloat16),
        in_specs=[smem] * 4 + [vmem] * 4,
        out_specs=vmem,
        scratch_shapes=[
            pltpu.VMEM((lat_dev + 2 * HALO, chans, ext_lanes), jnp.float32),
            pltpu.VMEM((lat_dev, G, S * G), jnp.bfloat16),
            pltpu.VMEM((S * G, CHUNK), jnp.bfloat16),
        ],
        compiler_params=params,
        name="disco",
    )(support_lat, support_lon, support_basis, support_value, turned, low, high, twice)
    mixed = lax.all_to_all(mixed, "chan", split_axis=0, concat_axis=0, tiled=True)
    table = jnp.asarray(fourier_rows(lon_count, chunks * CHUNK, mode_dev * devices, mode_dev))
    spectrum = pl.pallas_call(
        mlp_kernel,
        out_shape=jax.ShapeDtypeStruct((devices, PAD, LANES), jnp.bfloat16),
        in_specs=[vmem] * 4,
        out_specs=vmem,
        compiler_params=params,
        name="mlp",
    )(mixed, w_up, w_down, table)
    spectrum = lax.all_to_all(spectrum, ("lat", "chan"), split_axis=0, concat_axis=0, tiled=True)
    return pl.pallas_call(
        legendre_kernel,
        out_shape=jax.ShapeDtypeStruct((mode_dev, degrees, 4 * LANES), jnp.bfloat16),
        in_specs=[vmem] * 2,
        out_specs=vmem,
        scratch_shapes=[pltpu.VMEM((devices * PAD, LANES), jnp.float32)],
        compiler_params=params,
        name="legendre",
    )(spectrum, legendre)


def solution(mesh):
    in_specs = (
        P(("tm", "lat"), None, "chan"),
        P(None, "chan", None),
        P("lat", None),
        P("lat", None),
        P("lat", None),
        P("lat", None),
        P(),
        P(),
        P(("lat", "chan"), None, None),
    )
    out_specs = P(("tm", "lat", "chan"), None, None)
    return jax.shard_map(
        on_device, mesh=mesh, in_specs=in_specs, out_specs=out_specs, check_vma=False
    )
```

```python
import functools
import math

import jax
import jax.numpy as jnp
import ml_dtypes
import numpy as np
from jax import lax
from jax.experimental import pallas as pl
from jax.experimental.pallas import tpu as pltpu
from jax.sharding import PartitionSpec as P

G = 64
NB = 6
S = 9
HALO = 2
DLON = 4
LANES = 128
CHUNK = 384
PAD = 16
MESH = pl.DeviceIdType.MESH


def fourier_rows(lon_count, lon_pad, mode_count, mode_dev):
    lon = np.arange(lon_count, dtype=np.int64)
    mode = np.arange(mode_count, dtype=np.int64)
    phase = (lon[:, None] * mode[None, :]) % lon_count
    angle = phase.astype(np.float32) * np.float32(2.0 * math.pi / lon_count)
    scale = np.float32(math.sqrt(2.0 / lon_count))
    table = np.zeros((mode_count // mode_dev, PAD // 2, lon_pad), np.float32)
    pair = np.stack([np.cos(angle), -np.sin(angle)], axis=-1) * scale
    pair = pair.reshape(lon_count, mode_count // mode_dev, 2 * mode_dev)
    table[:, : 2 * mode_dev, :lon_count] = np.transpose(pair, (1, 2, 0))
    return table.reshape(-1, lon_pad).astype(ml_dtypes.bfloat16)


def spread(block, ext, row, lon_count):
    chans = block.shape[0]
    tiles = -(-lon_count // LANES)
    last = lon_count - (tiles - 1) * LANES
    lane = lax.broadcasted_iota(jnp.int32, (chans, LANES), 1)
    pieces = [block[:, t * LANES : min((t + 1) * LANES, lon_count)].astype(jnp.float32) for t in range(tiles)]
    if last < LANES:
        pieces[-1] = jnp.concatenate([pieces[-1], jnp.zeros((chans, LANES - last), jnp.float32)], axis=1)
    turned = [pltpu.roll(p, DLON, 1) for p in pieces]
    before = pltpu.roll(pieces[-1], (LANES - last + DLON) % LANES, 1)
    after = pltpu.roll(pieces[0], last + DLON, 1)
    for t in range(tiles):
        left = before if t == 0 else turned[t - 1]
        value = jnp.where(lane < DLON, left, turned[t])
        if t == tiles - 1:
            value = jnp.where(lane < last + DLON, value, jnp.where(lane < last + 2 * DLON, after, 0.0))
        ext[row, :, t * LANES : (t + 1) * LANES] = value.astype(ext.dtype)
    ext[row, :, tiles * LANES :] = jnp.zeros((chans, ext.shape[2] - tiles * LANES), ext.dtype)


def make_filters(row, basis, value, weight, filters):
    for pair in range(0, S, 2):
        parts = [
            weight[basis[row, tap]].astype(jnp.float32) * value[row, tap]
            for tap in range(pair, min(pair + 2, S))
        ]
        joined = parts[0] if len(parts) == 1 else jnp.concatenate(parts, axis=1)
        filters[row, :, pair * G : (pair + len(parts)) * G] = joined.astype(filters.dtype)


def disco_chunk(row, start, shift_lat, shift_lon, ext, filters, columns):
    lane = lax.broadcasted_iota(jnp.int32, (G, LANES), 1)
    for tap in range(S):
        source = row + HALO + shift_lat[row, tap]
        turn = DLON + shift_lon[row, tap]
        held = ext[source, :, pl.ds(start, CHUNK + LANES)]
        turned = [
            pltpu.roll(held[:, t * LANES : (t + 1) * LANES], LANES - turn, 1)
            for t in range(CHUNK // LANES + 1)
        ]
        for t in range(CHUNK // LANES):
            columns[tap * G : (tap + 1) * G, t * LANES : (t + 1) * LANES] = jnp.where(
                lane < LANES - turn, turned[t], turned[t + 1]
            ).astype(columns.dtype)
    return jnp.dot(filters[row], columns[...], preferred_element_type=jnp.float32)


def block_kernel(
    num_lat,
    num_chan,
    shift_lat,
    shift_lon,
    basis,
    value,
    fields,
    weight,
    w_up,
    w_down,
    table_hbm,
    legendre_hbm,
    out,
    own,
    halo,
    ext,
    filters,
    columns,
    mixed,
    gathered,
    up,
    down,
    table,
    legendre,
    total,
    sent,
    taken,
    wide,
    load_sem,
    halo_send,
    halo_recv,
    mix_send,
    mix_recv,
    spec_send,
    spec_recv,
):
    lat_dev, chans, lon_count = fields.shape
    chunks = mixed.shape[1]
    mode_dev, degrees, lats = legendre.shape
    devices = num_lat * num_chan
    half = lat_dev // 2
    band = lax.axis_index("lat")
    mine = lax.axis_index("chan")
    me = band * num_chan + mine
    core = lax.rem(band, 2)

    def device(index):
        return {"lat": lax.div(index, num_chan), "chan": lax.rem(index, num_chan)}

    loads = [
        pltpu.make_async_copy(table_hbm, table, load_sem.at[0]),
        pltpu.make_async_copy(legendre_hbm, legendre, load_sem.at[1]),
    ]
    for load in loads:
        load.start()
    barrier = pltpu.get_barrier_semaphore()

    def greet(step, carry):
        pl.semaphore_signal(
            barrier, inc=1, device_id=device(lax.rem(me + step, devices)), device_id_type=MESH
        )
        return carry

    lax.fori_loop(1, devices, greet, 0)
    pl.semaphore_wait(barrier, devices - 1)

    upward = pltpu.make_async_remote_copy(
        src_ref=fields.at[pl.ds(lat_dev - HALO, HALO)],
        dst_ref=halo.at[0],
        send_sem=halo_send.at[0],
        recv_sem=halo_recv.at[0],
        device_id={"lat": band + 1},
        device_id_type=MESH,
    )
    downward = pltpu.make_async_remote_copy(
        src_ref=fields.at[pl.ds(0, HALO)],
        dst_ref=halo.at[1],
        send_sem=halo_send.at[1],
        recv_sem=halo_recv.at[1],
        device_id={"lat": band - 1},
        device_id_type=MESH,
    )

    @pl.when(band < num_lat - 1)
    def _():
        upward.start()

    @pl.when(band > 0)
    def _():
        downward.start()

    for row in range(lat_dev):
        spread(fields[row], ext, HALO + row, lon_count)
        make_filters(row, basis, value, weight, filters)
    up[...] = w_up[...].T
    down[...] = w_down[...].T

    def disco_row(row, c):
        start = pl.multiple_of(c * CHUNK, LANES)
        acc = disco_chunk(row, start, shift_lat, shift_lon, ext, filters, columns)
        here = ext_own[row, :, pl.ds(start, CHUNK)].astype(jnp.float32)
        result = (here + acc).astype(mixed.dtype)

        @pl.when(row == mine)
        def _():
            gathered[c, mine] = result

        @pl.when(row != mine)
        def _():
            mixed[row, c] = result
            pltpu.make_async_remote_copy(
                src_ref=mixed.at[row, c],
                dst_ref=gathered.at[c, mine],
                send_sem=mix_send,
                recv_sem=mix_recv.at[c],
                device_id={"chan": row},
                device_id_type=MESH,
            ).start()

    ext_own = own
    for row in range(lat_dev):
        own[row, :, :lon_count] = fields[row]
        own[row, :, lon_count:] = jnp.zeros((chans, own.shape[2] - lon_count), own.dtype)
    for turn in range(2):
        side = 1 - core if turn == 0 else core
        present = jnp.where(side == 0, band > 0, band < num_lat - 1)

        @pl.when(present)
        def _():
            pltpu.make_async_copy(halo.at[side], halo.at[side], halo_recv.at[side]).wait()

        @pl.when(jnp.logical_not(present))
        def _():
            halo[side] = jnp.zeros(halo.shape[1:], halo.dtype)

        for r in range(HALO):
            spread(halo[side, r], ext, side * (HALO + lat_dev) + r, lon_count)

        def steps(step, carry):
            disco_row(side * half + lax.rem(step, half), lax.div(step, half))
            return carry

        lax.fori_loop(0, half * chunks, steps, 0)

    loads[0].wait()

    def mlp_part(c):
        pltpu.make_async_copy(
            gathered.at[c, pl.ds(0, num_chan - 1)],
            gathered.at[c, pl.ds(0, num_chan - 1)],
            mix_recv.at[c],
        ).wait()
        block = gathered[c].reshape(num_chan * chans, CHUNK)
        done = mlp_chunk(block, up[...], down[...])
        return lax.dot_general(
            table[:, pl.ds(pl.multiple_of(c * CHUNK, LANES), CHUNK)],
            done,
            (((1,), (1,)), ((), ())),
            preferred_element_type=jnp.float32,
        )

    total[...] = mlp_part(0)

    def mlp_step(c, carry):
        total[...] += mlp_part(c)
        return carry

    lax.fori_loop(1, chunks, mlp_step, 0)
    rows = PAD // 2
    for h in range(2):
        piece = total[:, h * LANES : (h + 1) * LANES].astype(jnp.bfloat16)
        sent[:, h * rows : (h + 1) * rows, :] = piece.reshape(devices, rows, LANES)

    def hand_out(step, carry):
        to = lax.rem(me + step, devices)
        pltpu.make_async_remote_copy(
            src_ref=sent.at[to],
            dst_ref=taken.at[me],
            send_sem=spec_send,
            recv_sem=spec_recv,
            device_id=device(to),
            device_id_type=MESH,
        ).start()
        return carry

    lax.fori_loop(1, devices, hand_out, 0)
    taken[me] = sent[me]
    loads[1].wait()
    degree = lax.broadcasted_iota(jnp.int32, (degrees, lats), 0)
    for m in range(mode_dev):
        kept = jnp.where(degree >= me * mode_dev + m, legendre[m].astype(jnp.float32), 0.0)
        legendre[m] = kept.astype(jnp.bfloat16)
    pltpu.make_async_copy(
        taken.at[pl.ds(0, devices - 1)], taken.at[pl.ds(0, devices - 1)], spec_recv
    ).wait()
    wide[...] = taken[...].astype(jnp.float32).reshape(devices * PAD, LANES)
    for m in range(mode_dev):
        picks = [h * rows + 2 * m + r for r in range(2) for h in range(2)]
        right = jnp.concatenate(
            [wide[pl.ds(j, devices, stride=PAD), :].astype(jnp.bfloat16) for j in picks], axis=1
        )
        out[m] = jnp.dot(legendre[m], right, preferred_element_type=jnp.float32).astype(out.dtype)
    pltpu.make_async_copy(mixed.at[pl.ds(0, lat_dev - 1)], mixed.at[pl.ds(0, lat_dev - 1)], mix_send).wait()
    pltpu.make_async_copy(sent.at[pl.ds(0, devices - 1)], sent.at[pl.ds(0, devices - 1)], spec_send).wait()

    @pl.when(band < num_lat - 1)
    def _():
        upward.wait_send()

    @pl.when(band > 0)
    def _():
        downward.wait_send()


def mlp_chunk(mixed, up, down):
    values = mixed.astype(jnp.float32)
    center = values - jnp.mean(values, axis=0, keepdims=True)
    variance = jnp.mean(center * center, axis=0, keepdims=True)
    normed = (center * lax.rsqrt(variance + 1e-05)).astype(jnp.bfloat16)
    lifted = jnp.dot(up, normed, preferred_element_type=jnp.float32)
    inner = math.sqrt(2.0 / math.pi) * (lifted + 0.044715 * (lifted * lifted * lifted))
    active = (0.5 * lifted * (1.0 + jnp.tanh(inner))).astype(jnp.bfloat16)
    lowered = jnp.dot(down, active, preferred_element_type=jnp.float32)
    return (values + lowered).astype(jnp.bfloat16)


def on_device(
    fields, disco_weight, support_lat, support_lon, support_basis, support_value, w_up, w_down, legendre
):
    lat_dev, lon_count, chans = fields.shape
    num_lat = lax.axis_size("lat")
    num_chan = lax.axis_size("chan")
    mode_dev, degrees, lats = legendre.shape
    devices = num_lat * num_chan
    chunks = -(-lon_count // CHUNK)
    lon_pad = chunks * CHUNK
    hidden = w_up.shape[1]
    smem = pl.BlockSpec(memory_space=pltpu.SMEM)
    vmem = pl.BlockSpec(memory_space=pltpu.VMEM)
    hbm = pl.BlockSpec(memory_space=pl.ANY)
    bf16, f32 = jnp.bfloat16, jnp.float32
    dma = pltpu.SemaphoreType.DMA
    table = jnp.asarray(fourier_rows(lon_count, lon_pad, mode_dev * devices, mode_dev))
    return pl.pallas_call(
        functools.partial(block_kernel, num_lat, num_chan),
        out_shape=jax.ShapeDtypeStruct((mode_dev, degrees, 4 * LANES), bf16),
        in_specs=[smem] * 4 + [vmem] * 4 + [hbm] * 2,
        out_specs=vmem,
        scratch_shapes=[
            pltpu.VMEM((lat_dev, chans, lon_pad), bf16),
            pltpu.VMEM((2, HALO, chans, lon_count), bf16),
            pltpu.VMEM((lat_dev + 2 * HALO, chans, lon_pad + LANES), f32),
            pltpu.VMEM((lat_dev, G, S * G), bf16),
            pltpu.VMEM((S * G, CHUNK), bf16),
            pltpu.VMEM((lat_dev, chunks, chans, CHUNK), bf16),
            pltpu.VMEM((chunks, num_chan, chans, CHUNK), bf16),
            pltpu.VMEM((hidden, num_chan * chans), bf16),
            pltpu.VMEM((num_chan * chans, hidden), bf16),
            pltpu.VMEM(table.shape, bf16),
            pltpu.VMEM(legendre.shape, bf16),
            pltpu.VMEM((devices * PAD // 2, num_chan * chans), f32),
            pltpu.VMEM((devices, PAD, LANES), bf16),
            pltpu.VMEM((devices, PAD, LANES), bf16),
            pltpu.VMEM((devices * PAD, LANES), f32),
            dma((2,)),
            dma((2,)),
            dma((2,)),
            dma,
            dma((chunks,)),
            dma,
            dma,
        ],
        compiler_params=pltpu.CompilerParams(
            collective_id=0, has_side_effects=True, vmem_limit_bytes=56 << 20
        ),
        name="block",
    )(
        support_lat,
        support_lon,
        support_basis,
        support_value,
        jnp.swapaxes(fields, 1, 2),
        disco_weight,
        w_up,
        w_down,
        table,
        legendre,
    )


def solution(mesh):
    in_specs = (
        P(("tm", "lat"), None, "chan"),
        P(None, "chan", None),
        P("lat", None),
        P("lat", None),
        P("lat", None),
        P("lat", None),
        P(),
        P(),
        P(("lat", "chan"), None, None),
    )
    out_specs = P(("tm", "lat", "chan"), None, None)
    return jax.shard_map(
        on_device, mesh=mesh, in_specs=in_specs, out_specs=out_specs, check_vma=False
    )
```

```python
import functools
import math

import jax
import jax.numpy as jnp
import ml_dtypes
import numpy as np
from jax import lax
from jax.experimental import pallas as pl
from jax.experimental.pallas import tpu as pltpu
from jax.sharding import PartitionSpec as P

G = 64
NB = 6
S = 9
HALO = 2
DLON = 4
LANES = 128
CHUNK = 384
PAD = 16
MESH = pl.DeviceIdType.MESH


def fourier_rows(lon_count, lon_pad, mode_count, mode_dev):
    lon = np.arange(lon_count, dtype=np.int64)
    mode = np.arange(mode_count, dtype=np.int64)
    phase = (lon[:, None] * mode[None, :]) % lon_count
    angle = phase.astype(np.float32) * np.float32(2.0 * math.pi / lon_count)
    scale = np.float32(math.sqrt(2.0 / lon_count))
    table = np.zeros((mode_count // mode_dev, PAD // 2, lon_pad), np.float32)
    pair = np.stack([np.cos(angle), -np.sin(angle)], axis=-1) * scale
    pair = pair.reshape(lon_count, mode_count // mode_dev, 2 * mode_dev)
    table[:, : 2 * mode_dev, :lon_count] = np.transpose(pair, (1, 2, 0))
    return table.reshape(-1, lon_pad).astype(ml_dtypes.bfloat16)


def spread(block, ext, row, lon_count):
    chans = block.shape[0]
    tiles = -(-lon_count // LANES)
    last = lon_count - (tiles - 1) * LANES
    lane = lax.broadcasted_iota(jnp.int32, (chans, LANES), 1)
    pieces = [block[:, t * LANES : min((t + 1) * LANES, lon_count)].astype(jnp.float32) for t in range(tiles)]
    if last < LANES:
        pieces[-1] = jnp.concatenate([pieces[-1], jnp.zeros((chans, LANES - last), jnp.float32)], axis=1)
    turned = [pltpu.roll(p, DLON, 1) for p in pieces]
    before = pltpu.roll(pieces[-1], (LANES - last + DLON) % LANES, 1)
    after = pltpu.roll(pieces[0], last + DLON, 1)
    for t in range(tiles):
        left = before if t == 0 else turned[t - 1]
        value = jnp.where(lane < DLON, left, turned[t])
        if t == tiles - 1:
            value = jnp.where(lane < last + DLON, value, jnp.where(lane < last + 2 * DLON, after, 0.0))
        ext[row, :, t * LANES : (t + 1) * LANES] = value.astype(ext.dtype)
    ext[row, :, tiles * LANES :] = jnp.zeros((chans, ext.shape[2] - tiles * LANES), ext.dtype)


def make_filters(row, basis, value, weight, filters):
    for pair in range(0, S, 2):
        parts = [
            weight[basis[row, tap]].astype(jnp.float32) * value[row, tap]
            for tap in range(pair, min(pair + 2, S))
        ]
        joined = parts[0] if len(parts) == 1 else jnp.concatenate(parts, axis=1)
        filters[row, :, pair * G : (pair + len(parts)) * G] = joined.astype(filters.dtype)


def disco_chunk(row, start, shift_lat, shift_lon, ext, filters, columns):
    lane = lax.broadcasted_iota(jnp.int32, (G, LANES), 1)
    for tap in range(S):
        source = row + HALO + shift_lat[row, tap]
        turn = DLON + shift_lon[row, tap]
        held = ext[source, :, pl.ds(start, CHUNK + LANES)]
        turned = [
            pltpu.roll(held[:, t * LANES : (t + 1) * LANES], LANES - turn, 1)
            for t in range(CHUNK // LANES + 1)
        ]
        for t in range(CHUNK // LANES):
            columns[tap * G : (tap + 1) * G, t * LANES : (t + 1) * LANES] = jnp.where(
                lane < LANES - turn, turned[t], turned[t + 1]
            ).astype(columns.dtype)
    return jnp.dot(filters[row], columns[...], preferred_element_type=jnp.float32)


def block_kernel(
    num_lat,
    num_chan,
    shift_lat,
    shift_lon,
    basis,
    value,
    fields_hbm,
    weight_hbm,
    up_hbm,
    down_hbm,
    table_hbm,
    taken,
    fields,
    weight,
    w_up,
    w_down,
    own,
    relay,
    halo,
    ext,
    filters,
    columns,
    mixed,
    gathered,
    up,
    down,
    table,
    total,
    sent,
    load_sem,
    halo_send,
    halo_recv,
    relay_sent,
    relay_recv,
    mix_send,
    mix_recv,
    spec_send,
    spec_recv,
):
    lat_dev, chans, lon_count = fields.shape
    chunks = mixed.shape[1]
    devices = num_lat * num_chan
    half = lat_dev // 2
    band = lax.axis_index("lat")
    mine = lax.axis_index("chan")
    me = band * num_chan + mine
    core = lax.rem(band, 2)

    def device(index):
        return {"lat": lax.div(index, num_chan), "chan": lax.rem(index, num_chan)}

    barrier = pltpu.get_barrier_semaphore()

    def greet(step, carry):
        pl.semaphore_signal(
            barrier, inc=1, device_id=device(lax.rem(me + step, devices)), device_id_type=MESH
        )
        return carry

    lax.fori_loop(1, devices, greet, 0)
    pairs = [
        (fields_hbm, fields),
        (weight_hbm, weight),
        (up_hbm, w_up),
        (down_hbm, w_down),
        (table_hbm, table),
    ]
    loads = [pltpu.make_async_copy(a, b, load_sem.at[i]) for i, (a, b) in enumerate(pairs)]
    for load in loads:
        load.start()
    pl.semaphore_wait(barrier, devices - 1)

    sends = [
        [
            pltpu.make_async_remote_copy(
                src_ref=fields_hbm.at[lat_dev - 1 - step if side == 0 else step],
                dst_ref=halo.at[side, HALO - 1 - step if side == 0 else step],
                send_sem=halo_send.at[side, step],
                recv_sem=halo_recv.at[side, step],
                device_id={"lat": band + 1 if side == 0 else band - 1},
                device_id_type=MESH,
            )
            for step in range(HALO)
        ]
        for side in range(2)
    ]

    seam = num_lat // 2
    ring = seam // 2
    high_z = lax.div(band, seam)
    place = lax.rem(lax.div(band, 2), ring)
    per_lat = ring // HALO
    width = chans // per_lat
    at_seam = jnp.logical_or(band == seam - 1, band == seam)
    is_first = high_z != core

    def part_of(index):
        return lax.div(index, per_lat), pl.ds(pl.multiple_of(lax.rem(index, per_lat) * width, width), width)

    def relay_send(src, sem, to):
        return pltpu.make_async_remote_copy(
            src_ref=src, dst_ref=relay, send_sem=sem, recv_sem=relay_recv,
            device_id={"lat": to}, device_id_type=MESH,
        )

    @pl.when(jnp.logical_and(band < num_lat - 1, band != seam - 1))
    def _():
        for send in sends[0]:
            send.start()

    @pl.when(jnp.logical_and(band > 0, band != seam))
    def _():
        for send in sends[1]:
            send.start()

    for side, source in ((0, seam - 1), (1, seam)):
        @pl.when(band == source)
        def _():
            def start_part(index, carry):
                step, rows = part_of(index)
                to = 2 * index + 1 if side == 0 else seam + 2 * index
                other = source + seam if side == 0 else source - seam
                to = jnp.where(to == source, other, to)
                lat_row = lat_dev - 1 - step if side == 0 else step
                relay_send(fields_hbm.at[lat_row, rows], halo_send.at[side, step], to).start()
                return carry

            lax.fori_loop(0, ring, start_part, 0)

    for load in loads[:4]:
        load.wait()
    for row in range(lat_dev):
        spread(fields[row], ext, HALO + row, lon_count)
        make_filters(row, basis, value, weight, filters)
    @pl.when(jnp.logical_and(is_first, jnp.logical_not(at_seam)))
    def _():
        pltpu.make_async_copy(relay, relay, relay_recv).wait()
        relay_send(relay, relay_sent, jnp.where(band < seam, band + seam, band - seam)).start()

    up[...] = w_up[...].T
    down[...] = w_down[...].T

    def disco_row(row, to, c):
        start = pl.multiple_of(c * CHUNK, LANES)
        acc = disco_chunk(row, start, shift_lat, shift_lon, ext, filters, columns)
        here = own[row, :, pl.ds(start, CHUNK)].astype(jnp.float32)
        result = (here + acc).astype(mixed.dtype)

        @pl.when(to == mine)
        def _():
            gathered[c, mine] = result

        @pl.when(to != mine)
        def _():
            mixed[to, c] = result
            pltpu.make_async_remote_copy(
                src_ref=mixed.at[to, c],
                dst_ref=gathered.at[c, mine],
                send_sem=mix_send,
                recv_sem=mix_recv.at[c],
                device_id={"chan": to},
                device_id_type=MESH,
            ).start()

    for row in range(lat_dev):
        own[row, :, :lon_count] = fields[row]
        own[row, :, lon_count:] = jnp.zeros((chans, own.shape[2] - lon_count), own.dtype)
    first = 1 - core
    for turn in range(2):
        side = first if turn == 0 else 1 - first
        if turn == 1:

            @pl.when(jnp.logical_not(is_first))
            def _():
                pltpu.make_async_copy(relay, relay, relay_recv).wait()
                step, rows = part_of(place)
                to_side = 1 - core
                edge = jnp.where(core == 1, HALO - 1 - step, step)
                pltpu.make_async_remote_copy(
                    src_ref=relay,
                    dst_ref=halo.at[to_side, edge, rows],
                    send_sem=relay_sent,
                    recv_sem=halo_recv.at[to_side, step],
                    device_id={"lat": jnp.where(core == 1, seam, seam - 1)},
                    device_id_type=MESH,
                ).start()

        present = jnp.where(side == 0, band > 0, band < num_lat - 1)
        for step in range(HALO):
            edge = jnp.where(side == 0, HALO - 1 - step, step)
            row = jnp.where(side == 0, half - 1 - step, half + step)
            order = jnp.where(core == 0, step, half - 1 - step)
            to = order * (num_chan - 1) if turn == 0 else order + 1

            @pl.when(present)
            def _():
                arrived = halo.at[side, edge]
                pltpu.make_async_copy(arrived, arrived, halo_recv.at[side, step]).wait()

            @pl.when(jnp.logical_not(present))
            def _():
                halo[side, edge] = jnp.zeros(halo.shape[2:], halo.dtype)

            spread(halo[side, edge], ext, side * (HALO + lat_dev) + edge, lon_count)

            def steps(c, carry):
                disco_row(row, to, c)
                return carry

            lax.fori_loop(0, chunks, steps, 0)

    loads[4].wait()

    def mlp_part(c):
        pltpu.make_async_copy(
            gathered.at[c, pl.ds(0, num_chan - 1)],
            gathered.at[c, pl.ds(0, num_chan - 1)],
            mix_recv.at[c],
        ).wait()
        block = gathered[c].reshape(num_chan * chans, CHUNK)
        done = mlp_chunk(block, up[...], down[...])
        return lax.dot_general(
            table[:, pl.ds(pl.multiple_of(c * CHUNK, LANES), CHUNK)],
            done,
            (((1,), (1,)), ((), ())),
            preferred_element_type=jnp.float32,
        )

    total[...] = mlp_part(0)

    def mlp_step(c, carry):
        total[...] += mlp_part(c)
        return carry

    lax.fori_loop(1, chunks, mlp_step, 0)
    rows = PAD // 2
    for h in range(2):
        piece = total[:, h * LANES : (h + 1) * LANES].astype(jnp.bfloat16)
        sent[:, h * rows : (h + 1) * rows, :] = piece.reshape(devices, rows, LANES)

    at_end = jnp.logical_or(mine == 0, mine == num_chan - 1)
    order = jnp.where(at_end, lax.div(mine, num_chan - 1), mine - 1)
    step_here = jnp.where(core == 0, order, half - 1 - order)
    side_here = jnp.where(at_end, first, 1 - first)
    lat = band * lat_dev + jnp.where(side_here == 0, half - 1 - step_here, half + step_here)

    def hand_out(step, carry):
        to = lax.rem(me + step, devices)
        pltpu.make_async_remote_copy(
            src_ref=sent.at[to],
            dst_ref=taken.at[lat],
            send_sem=spec_send,
            recv_sem=spec_recv,
            device_id=device(to),
            device_id_type=MESH,
        ).start()
        return carry

    lax.fori_loop(1, devices, hand_out, 0)
    keep = pltpu.make_async_copy(sent.at[me], taken.at[lat], load_sem.at[5])
    keep.start()
    keep.wait()
    pltpu.make_async_copy(
        taken.at[pl.ds(0, devices - 1)], taken.at[pl.ds(0, devices - 1)], spec_recv
    ).wait()
    pltpu.make_async_copy(mixed.at[pl.ds(0, lat_dev - 1)], mixed.at[pl.ds(0, lat_dev - 1)], mix_send).wait()
    pltpu.make_async_copy(sent.at[pl.ds(0, devices - 1)], sent.at[pl.ds(0, devices - 1)], spec_send).wait()

    @pl.when(jnp.logical_not(at_seam))
    def _():
        pltpu.make_async_copy(relay, relay, relay_sent).wait()

    @pl.when(band < num_lat - 1)
    def _():
        for send in sends[0]:
            send.wait_send()

    @pl.when(band > 0)
    def _():
        for send in sends[1]:
            send.wait_send()


def mlp_chunk(mixed, up, down):
    values = mixed.astype(jnp.float32)
    center = values - jnp.mean(values, axis=0, keepdims=True)
    variance = jnp.mean(center * center, axis=0, keepdims=True)
    normed = (center * lax.rsqrt(variance + 1e-05)).astype(jnp.bfloat16)
    lifted = jnp.dot(up, normed, preferred_element_type=jnp.float32)
    inner = math.sqrt(2.0 / math.pi) * (lifted + 0.044715 * (lifted * lifted * lifted))
    active = (0.5 * lifted * (1.0 + jnp.tanh(inner))).astype(jnp.bfloat16)
    lowered = jnp.dot(down, active, preferred_element_type=jnp.float32)
    return (values + lowered).astype(jnp.bfloat16)


def legendre_kernel(taken_hbm, legendre_hbm, out_hbm, taken, legendre, out, wide, load_sem, out_sem):
    mode_dev, degrees, lats = legendre.shape
    rows = PAD // 2
    loads = [
        pltpu.make_async_copy(legendre_hbm, legendre, load_sem.at[0]),
        pltpu.make_async_copy(taken_hbm, taken, load_sem.at[1]),
    ]
    for load in loads:
        load.start()
    me = lax.axis_index("lat") * lax.axis_size("chan") + lax.axis_index("chan")
    degree = lax.broadcasted_iota(jnp.int32, (degrees, lats), 0)
    loads[0].wait()
    for m in range(mode_dev):
        kept = jnp.where(degree >= me * mode_dev + m, legendre[m].astype(jnp.float32), 0.0)
        legendre[m] = kept.astype(jnp.bfloat16)
    loads[1].wait()
    wide[...] = taken[...].astype(jnp.float32).reshape(lats * PAD, LANES)
    stores = [pltpu.make_async_copy(out.at[m], out_hbm.at[m], out_sem.at[m]) for m in range(mode_dev)]
    for m in range(mode_dev):
        picks = [h * rows + 2 * m + r for r in range(2) for h in range(2)]
        right = jnp.concatenate(
            [wide[pl.ds(j, lats, stride=PAD), :].astype(jnp.bfloat16) for j in picks], axis=1
        )
        out[m] = jnp.dot(legendre[m], right, preferred_element_type=jnp.float32).astype(out.dtype)
        stores[m].start()
    for store in stores:
        store.wait()


def on_device(
    fields, disco_weight, support_lat, support_lon, support_basis, support_value, w_up, w_down, legendre
):
    lat_dev, lon_count, chans = fields.shape
    num_lat = lax.axis_size("lat")
    num_chan = lax.axis_size("chan")
    mode_dev, degrees, lats = legendre.shape
    devices = num_lat * num_chan
    chunks = -(-lon_count // CHUNK)
    lon_pad = chunks * CHUNK
    hidden = w_up.shape[1]
    smem = pl.BlockSpec(memory_space=pltpu.SMEM)
    hbm = pl.BlockSpec(memory_space=pltpu.HBM)
    bf16, f32 = jnp.bfloat16, jnp.float32
    dma = pltpu.SemaphoreType.DMA
    table = jnp.asarray(fourier_rows(lon_count, lon_pad, mode_dev * devices, mode_dev))
    taken = pl.pallas_call(
        functools.partial(block_kernel, num_lat, num_chan),
        out_shape=jax.ShapeDtypeStruct((devices, PAD, LANES), bf16),
        in_specs=[smem] * 4 + [hbm] * 5,
        out_specs=hbm,
        scratch_shapes=[
            pltpu.VMEM((lat_dev, chans, lon_count), bf16),
            pltpu.VMEM(disco_weight.shape, bf16),
            pltpu.VMEM(w_up.shape, bf16),
            pltpu.VMEM(w_down.shape, bf16),
            pltpu.VMEM((lat_dev, chans, lon_pad), bf16),
            pltpu.VMEM((chans * HALO * 4 // num_lat, lon_count), bf16),
            pltpu.VMEM((2, HALO, chans, lon_count), bf16),
            pltpu.VMEM((lat_dev + 2 * HALO, chans, lon_pad + LANES), f32),
            pltpu.VMEM((lat_dev, G, S * G), bf16),
            pltpu.VMEM((S * G, CHUNK), bf16),
            pltpu.VMEM((lat_dev, chunks, chans, CHUNK), bf16),
            pltpu.VMEM((chunks, num_chan, chans, CHUNK), bf16),
            pltpu.VMEM((hidden, num_chan * chans), bf16),
            pltpu.VMEM((num_chan * chans, hidden), bf16),
            pltpu.VMEM(table.shape, bf16),
            pltpu.VMEM((devices * PAD // 2, num_chan * chans), f32),
            pltpu.VMEM((devices, PAD, LANES), bf16),
            dma((6,)),
            dma((2, HALO)),
            dma((2, HALO)),
            dma,
            dma,
            dma,
            dma((chunks,)),
            dma,
            dma,
        ],
        compiler_params=pltpu.CompilerParams(
            collective_id=0, has_side_effects=True, vmem_limit_bytes=56 << 20
        ),
        name="block",
    )(
        support_lat,
        support_lon,
        support_basis,
        support_value,
        jnp.swapaxes(fields, 1, 2),
        disco_weight,
        w_up,
        w_down,
        table,
    )
    return pl.pallas_call(
        legendre_kernel,
        out_shape=jax.ShapeDtypeStruct((mode_dev, degrees, 4 * LANES), bf16),
        in_specs=[hbm] * 2,
        out_specs=hbm,
        scratch_shapes=[
            pltpu.VMEM((devices, PAD, LANES), bf16),
            pltpu.VMEM(legendre.shape, bf16),
            pltpu.VMEM((mode_dev, degrees, 4 * LANES), bf16),
            pltpu.VMEM((devices * PAD, LANES), f32),
            dma((2,)),
            dma((mode_dev,)),
        ],
        compiler_params=pltpu.CompilerParams(vmem_limit_bytes=56 << 20),
        name="legendre",
    )(taken, legendre)


def solution(mesh):
    in_specs = (
        P(("tm", "lat"), None, "chan"),
        P(None, "chan", None),
        P("lat", None),
        P("lat", None),
        P("lat", None),
        P("lat", None),
        P(),
        P(),
        P(("lat", "chan"), None, None),
    )
    out_specs = P(("tm", "lat", "chan"), None, None)
    return jax.shard_map(
        on_device, mesh=mesh, in_specs=in_specs, out_specs=out_specs, check_vma=False
    )
```

```python
import functools
import math

import jax
import jax.numpy as jnp
import ml_dtypes
import numpy as np
from jax import lax
from jax.experimental import pallas as pl
from jax.experimental.pallas import tpu as pltpu
from jax.sharding import PartitionSpec as P

G = 64
NB = 6
S = 9
HALO = 2
DLON = 4
LANES = 128
CHUNK = 384
MESH = pl.DeviceIdType.MESH


def fourier_rows(lon_count, lon_pad, mode_count, mode_dev):
    lon = np.arange(lon_count, dtype=np.int64)
    mode = np.arange(mode_count, dtype=np.int64)
    phase = (lon[:, None] * mode[None, :]) % lon_count
    angle = phase.astype(np.float32) * np.float32(2.0 * math.pi / lon_count)
    scale = np.float32(math.sqrt(2.0 / lon_count))
    table = np.zeros((2 * mode_dev, mode_count // mode_dev, lon_pad), np.float32)
    pair = np.stack([np.cos(angle), -np.sin(angle)], axis=-1) * scale
    pair = pair.reshape(lon_count, mode_count // mode_dev, 2 * mode_dev)
    table[:, :, :lon_count] = np.transpose(pair, (2, 1, 0))
    return table.reshape(-1, lon_pad).astype(ml_dtypes.bfloat16)


def spread(block, ext, row, lon_count):
    chans = block.shape[0]
    tiles = -(-lon_count // LANES)
    last = lon_count - (tiles - 1) * LANES
    lane = lax.broadcasted_iota(jnp.int32, (chans, LANES), 1)
    pieces = [block[:, t * LANES : min((t + 1) * LANES, lon_count)].astype(jnp.float32) for t in range(tiles)]
    if last < LANES:
        pieces[-1] = jnp.concatenate([pieces[-1], jnp.zeros((chans, LANES - last), jnp.float32)], axis=1)
    turned = [pltpu.roll(p, DLON, 1) for p in pieces]
    before = pltpu.roll(pieces[-1], (LANES - last + DLON) % LANES, 1)
    after = pltpu.roll(pieces[0], last + DLON, 1)
    for t in range(tiles):
        left = before if t == 0 else turned[t - 1]
        value = jnp.where(lane < DLON, left, turned[t])
        if t == tiles - 1:
            value = jnp.where(lane < last + DLON, value, jnp.where(lane < last + 2 * DLON, after, 0.0))
        ext[row, :, t * LANES : (t + 1) * LANES] = value.astype(ext.dtype)
    ext[row, :, tiles * LANES :] = jnp.zeros((chans, ext.shape[2] - tiles * LANES), ext.dtype)


def make_filters(row, basis, value, weight, filters):
    for pair in range(0, S, 2):
        parts = [
            weight[basis[row, tap]].astype(jnp.float32) * value[row, tap]
            for tap in range(pair, min(pair + 2, S))
        ]
        joined = parts[0] if len(parts) == 1 else jnp.concatenate(parts, axis=1)
        filters[row, :, pair * G : (pair + len(parts)) * G] = joined.astype(filters.dtype)


def disco_chunk(row, start, shift_lat, shift_lon, ext, filters, columns):
    lane = lax.broadcasted_iota(jnp.int32, (G, LANES), 1)
    for tap in range(S):
        source = row + HALO + shift_lat[row, tap]
        turn = DLON + shift_lon[row, tap]
        held = ext[source, :, pl.ds(start, CHUNK + LANES)]
        turned = [
            pltpu.roll(held[:, t * LANES : (t + 1) * LANES], LANES - turn, 1)
            for t in range(CHUNK // LANES + 1)
        ]
        for t in range(CHUNK // LANES):
            columns[tap * G : (tap + 1) * G, t * LANES : (t + 1) * LANES] = jnp.where(
                lane < LANES - turn, turned[t], turned[t + 1]
            ).astype(columns.dtype)
    return jnp.dot(filters[row], columns[...], preferred_element_type=jnp.float32)


def block_kernel(
    num_lat,
    num_chan,
    shift_lat,
    shift_lon,
    basis,
    value,
    fields_hbm,
    weight_hbm,
    up_hbm,
    down_hbm,
    table_hbm,
    taken,
    fields,
    weight,
    w_up,
    w_down,
    own,
    relay,
    halo,
    ext,
    filters,
    columns,
    mixed,
    gathered,
    rest_mixed,
    rest,
    up,
    down,
    table,
    total,
    wide,
    sent,
    load_sem,
    halo_send,
    halo_recv,
    relay_sent,
    relay_recv,
    mix_send,
    last_send,
    rest_send,
    mix_recv,
    rest_recv,
    spec_send,
    spec_recv,
):
    lat_dev, chans, lon_count = fields.shape
    chunks = mixed.shape[1]
    devices = num_lat * num_chan
    half = lat_dev // 2
    per_device = sent.shape[1] * sent.shape[2]
    band = lax.axis_index("lat")
    mine = lax.axis_index("chan")
    me = band * num_chan + mine
    core = lax.rem(band, 2)

    barrier = pltpu.get_barrier_semaphore()

    def greet(band_to, mine_to):
        pl.semaphore_signal(
            barrier, inc=1, device_id={"lat": band_to, "chan": mine_to}, device_id_type=MESH
        )

    for step in range(1, num_chan):
        greet(band, lax.rem(mine + step, num_chan))

    def greet_band(step, carry):
        for to in range(num_chan):
            greet(lax.rem(band + step, num_lat), to)
        return carry

    lax.fori_loop(1, num_lat, greet_band, 0)
    pairs = [
        (fields_hbm, fields),
        (weight_hbm, weight),
        (up_hbm, w_up),
        (down_hbm, w_down),
        (table_hbm, table),
    ]
    loads = [pltpu.make_async_copy(a, b, load_sem.at[i]) for i, (a, b) in enumerate(pairs)]
    for load in loads:
        load.start()
    pl.semaphore_wait(barrier, devices - 1)

    sends = [
        [
            pltpu.make_async_remote_copy(
                src_ref=fields_hbm.at[lat_dev - 1 - step if side == 0 else step],
                dst_ref=halo.at[side, HALO - 1 - step if side == 0 else step],
                send_sem=halo_send.at[side, step],
                recv_sem=halo_recv.at[side, step],
                device_id={"lat": band + 1 if side == 0 else band - 1},
                device_id_type=MESH,
            )
            for step in range(HALO)
        ]
        for side in range(2)
    ]

    seam = num_lat // 2
    ring = seam // 2
    high_z = lax.div(band, seam)
    place = lax.rem(lax.div(band, 2), ring)
    per_lat = ring // HALO
    width = chans // per_lat
    at_seam = jnp.logical_or(band == seam - 1, band == seam)
    is_first = high_z != core

    def part_of(index):
        return lax.div(index, per_lat), pl.ds(pl.multiple_of(lax.rem(index, per_lat) * width, width), width)

    def relay_send(src, sem, to):
        return pltpu.make_async_remote_copy(
            src_ref=src, dst_ref=relay, send_sem=sem, recv_sem=relay_recv,
            device_id={"lat": to}, device_id_type=MESH,
        )

    @pl.when(jnp.logical_and(band < num_lat - 1, band != seam - 1))
    def _():
        for send in sends[0]:
            send.start()

    @pl.when(jnp.logical_and(band > 0, band != seam))
    def _():
        for send in sends[1]:
            send.start()

    for side, source in ((0, seam - 1), (1, seam)):
        @pl.when(band == source)
        def _():
            def start_part(index, carry):
                step, rows = part_of(index)
                to = 2 * index + 1 if side == 0 else seam + 2 * index
                other = source + seam if side == 0 else source - seam
                to = jnp.where(to == source, other, to)
                lat_row = lat_dev - 1 - step if side == 0 else step
                relay_send(fields_hbm.at[lat_row, rows], halo_send.at[side, step], to).start()
                return carry

            lax.fori_loop(0, ring, start_part, 0)

    for load in loads[:2]:
        load.wait()
    for row in range(lat_dev):
        spread(fields[row], ext, HALO + row, lon_count)
        make_filters(row, basis, value, weight, filters)

    left = lon_count % LANES
    whole = lon_count - (chunks - 1) * CHUNK - left
    groups = LANES // left
    tall = chans // groups

    def pack(block):
        return jnp.concatenate(
            [block[g * tall : (g + 1) * tall, whole : whole + left] for g in range(groups)], axis=1
        )

    def unpack(packed):
        value = packed.astype(jnp.float32)
        turned = [value] + [pltpu.roll(value, LANES - g * left, 1) for g in range(1, groups)]
        return jnp.concatenate([t.astype(packed.dtype) for t in turned], axis=0)

    def mix_copy(src, dst, send_sem, recv_sem, to):
        return pltpu.make_async_remote_copy(
            src_ref=src, dst_ref=dst, send_sem=send_sem, recv_sem=recv_sem,
            device_id={"chan": to}, device_id_type=MESH,
        )

    def disco_row(row, to, c):
        start = pl.multiple_of(c * CHUNK, LANES)
        acc = disco_chunk(row, start, shift_lat, shift_lon, ext, filters, columns)
        here = own[row, :, pl.ds(start, CHUNK)].astype(jnp.float32)
        result = (here + acc).astype(mixed.dtype)

        @pl.when(to == mine)
        def _():
            gathered[c, mine] = result

            @pl.when(c == chunks - 1)
            def _():
                rest[mine] = pack(result)

        @pl.when(to != mine)
        def _():
            mixed[to, c] = result

            @pl.when(c < chunks - 1)
            def _():
                mix_copy(mixed.at[to, c], gathered.at[c, mine], mix_send, mix_recv.at[c], to).start()

            @pl.when(c == chunks - 1)
            def _():
                rest_mixed[to] = pack(result)
                src = mixed.at[to, chunks - 1, :, pl.ds(0, whole)]
                dst = gathered.at[chunks - 1, mine, :, pl.ds(0, whole)]
                mix_copy(src, dst, last_send, mix_recv.at[chunks - 1], to).start()
                mix_copy(rest_mixed.at[to], rest.at[mine], rest_send, rest_recv, to).start()

    for row in range(lat_dev):
        own[row, :, :lon_count] = fields[row]
        own[row, :, lon_count:] = jnp.zeros((chans, own.shape[2] - lon_count), own.dtype)
    first = 1 - core
    for turn in range(2):
        side = first if turn == 0 else 1 - first
        if turn == 1:

            @pl.when(jnp.logical_not(is_first))
            def _():
                pltpu.make_async_copy(relay, relay, relay_recv).wait()
                step, rows = part_of(place)
                to_side = 1 - core
                edge = jnp.where(core == 1, HALO - 1 - step, step)
                pltpu.make_async_remote_copy(
                    src_ref=relay,
                    dst_ref=halo.at[to_side, edge, rows],
                    send_sem=relay_sent,
                    recv_sem=halo_recv.at[to_side, step],
                    device_id={"lat": jnp.where(core == 1, seam, seam - 1)},
                    device_id_type=MESH,
                ).start()

        present = jnp.where(side == 0, band > 0, band < num_lat - 1)
        for step in range(HALO):
            edge = jnp.where(side == 0, HALO - 1 - step, step)
            row = jnp.where(side == 0, half - 1 - step, half + step)
            order = jnp.where(core == 0, step, half - 1 - step)
            to = order * (num_chan - 1) if turn == 0 else order + 1

            @pl.when(present)
            def _():
                arrived = halo.at[side, edge]
                pltpu.make_async_copy(arrived, arrived, halo_recv.at[side, step]).wait()

            @pl.when(jnp.logical_not(present))
            def _():
                halo[side, edge] = jnp.zeros(halo.shape[2:], halo.dtype)

            spread(halo[side, edge], ext, side * (HALO + lat_dev) + edge, lon_count)

            def steps(c, carry):
                disco_row(row, to, c)
                return carry

            lax.fori_loop(0, chunks, steps, 0)
            if turn == 0 and step == 0:

                @pl.when(jnp.logical_and(is_first, jnp.logical_not(at_seam)))
                def _():
                    pltpu.make_async_copy(relay, relay, relay_recv).wait()
                    relay_send(relay, relay_sent, jnp.where(band < seam, band + seam, band - seam)).start()

    for load in loads[2:5]:
        load.wait()
    up[...] = w_up[...].T
    down[...] = w_down[...].T

    def wait_for(ref, sem):
        pltpu.make_async_copy(ref, ref, sem).wait()

    def mlp_part(block, c):
        done = mlp_chunk(block, up[...], down[...])
        wide_lanes = block.shape[1]
        return lax.dot_general(
            table[:, pl.ds(pl.multiple_of(c * CHUNK, LANES), wide_lanes)],
            done,
            (((1,), (1,)), ((), ())),
            preferred_element_type=jnp.float32,
        )

    total[...] = jnp.zeros(total.shape, total.dtype)

    def mlp_step(c, carry):
        wait_for(gathered.at[c, pl.ds(0, num_chan - 1)], mix_recv.at[c])
        total[...] += mlp_part(gathered[c].reshape(num_chan * chans, CHUNK), c)
        return carry

    lax.fori_loop(0, chunks - 1, mlp_step, 0)
    wait_for(gathered.at[chunks - 1, pl.ds(0, num_chan - 1), :, pl.ds(0, whole)], mix_recv.at[chunks - 1])
    wait_for(rest.at[pl.ds(0, num_chan - 1)], rest_recv)
    block = jnp.concatenate([gathered[chunks - 1, p, :, :whole] for p in range(num_chan)], axis=0)
    tail = jnp.concatenate([unpack(rest[p]) for p in range(num_chan)], axis=0)
    total[...] += mlp_part(jnp.concatenate([block, tail], axis=1), chunks - 1)
    for j in range(per_device // 2):
        for h in range(2):
            piece = total[j * devices : (j + 1) * devices, h * LANES : (h + 1) * LANES]
            wide[pl.ds(2 * j + h, devices, stride=per_device), :] = piece
    sent[...] = wide[...].reshape(sent.shape).astype(sent.dtype)

    at_end = jnp.logical_or(mine == 0, mine == num_chan - 1)
    order = jnp.where(at_end, lax.div(mine, num_chan - 1), mine - 1)
    step_here = jnp.where(core == 0, order, half - 1 - order)
    side_here = jnp.where(at_end, first, 1 - first)
    lat = band * lat_dev + jnp.where(side_here == 0, half - 1 - step_here, half + step_here)

    def hand_out(band_to, mine_to):
        pltpu.make_async_remote_copy(
            src_ref=sent.at[band_to * num_chan + mine_to],
            dst_ref=taken.at[lat],
            send_sem=spec_send,
            recv_sem=spec_recv,
            device_id={"lat": band_to, "chan": mine_to},
            device_id_type=MESH,
        ).start()

    def hand_out_band(step, carry):
        for to in range(num_chan):
            hand_out(lax.rem(band + step, num_lat), to)
        return carry

    lax.fori_loop(1, num_lat, hand_out_band, 0)
    for step in range(1, num_chan):
        hand_out(band, lax.rem(mine + step, num_chan))
    keep = pltpu.make_async_copy(sent.at[me], taken.at[lat], load_sem.at[5])
    keep.start()
    keep.wait()
    pltpu.make_async_copy(
        taken.at[pl.ds(0, devices - 1)], taken.at[pl.ds(0, devices - 1)], spec_recv
    ).wait()
    wait_for(mixed.at[pl.ds(0, lat_dev - 1), pl.ds(0, chunks - 1)], mix_send)
    wait_for(mixed.at[pl.ds(0, lat_dev - 1), chunks - 1, :, pl.ds(0, whole)], last_send)
    wait_for(rest_mixed.at[pl.ds(0, lat_dev - 1)], rest_send)
    pltpu.make_async_copy(sent.at[pl.ds(0, devices - 1)], sent.at[pl.ds(0, devices - 1)], spec_send).wait()

    @pl.when(jnp.logical_not(at_seam))
    def _():
        pltpu.make_async_copy(relay, relay, relay_sent).wait()

    @pl.when(band < num_lat - 1)
    def _():
        for send in sends[0]:
            send.wait_send()

    @pl.when(band > 0)
    def _():
        for send in sends[1]:
            send.wait_send()


def mlp_chunk(mixed, up, down):
    values = mixed.astype(jnp.float32)
    center = values - jnp.mean(values, axis=0, keepdims=True)
    variance = jnp.mean(center * center, axis=0, keepdims=True)
    normed = (center * lax.rsqrt(variance + 1e-05)).astype(jnp.bfloat16)
    lifted = jnp.dot(up, normed, preferred_element_type=jnp.float32)
    inner = math.sqrt(2.0 / math.pi) * (lifted + 0.044715 * (lifted * lifted * lifted))
    active = (0.5 * lifted * (1.0 + jnp.tanh(inner))).astype(jnp.bfloat16)
    lowered = jnp.dot(down, active, preferred_element_type=jnp.float32)
    return (values + lowered).astype(jnp.bfloat16)


def legendre_kernel(taken_hbm, legendre_hbm, out_hbm, taken, legendre, out, wide, load_sem, out_sem):
    mode_dev, degrees, lats = legendre.shape
    loads = [
        pltpu.make_async_copy(legendre_hbm, legendre, load_sem.at[0]),
        pltpu.make_async_copy(taken_hbm, taken, load_sem.at[1]),
    ]
    for load in loads:
        load.start()
    me = lax.axis_index("lat") * lax.axis_size("chan") + lax.axis_index("chan")
    degree = lax.broadcasted_iota(jnp.int32, (degrees, lats), 0)
    loads[0].wait()
    for m in range(mode_dev):
        kept = jnp.where(degree >= me * mode_dev + m, legendre[m].astype(jnp.float32), 0.0)
        legendre[m] = kept.astype(jnp.bfloat16)
    loads[1].wait()
    wide[...] = taken[...].astype(jnp.float32).reshape(wide.shape)
    each = wide.shape[0] // lats
    per_mode = each // mode_dev
    stores = [pltpu.make_async_copy(out.at[m], out_hbm.at[m], out_sem.at[m]) for m in range(mode_dev)]
    for m in range(mode_dev):
        right = jnp.concatenate(
            [
                wide[pl.ds(m * per_mode + j, lats, stride=each), :].astype(jnp.bfloat16)
                for j in range(per_mode)
            ],
            axis=1,
        )
        out[m] = jnp.dot(legendre[m], right, preferred_element_type=jnp.float32).astype(out.dtype)
        stores[m].start()
    for store in stores:
        store.wait()


def on_device(
    fields, disco_weight, support_lat, support_lon, support_basis, support_value, w_up, w_down, legendre
):
    lat_dev, lon_count, chans = fields.shape
    num_lat = lax.axis_size("lat")
    num_chan = lax.axis_size("chan")
    mode_dev, degrees, lats = legendre.shape
    devices = num_lat * num_chan
    chunks = -(-lon_count // CHUNK)
    lon_pad = chunks * CHUNK
    hidden = w_up.shape[1]
    smem = pl.BlockSpec(memory_space=pltpu.SMEM)
    hbm = pl.BlockSpec(memory_space=pltpu.HBM)
    bf16, f32 = jnp.bfloat16, jnp.float32
    dma = pltpu.SemaphoreType.DMA
    packet = (devices, mode_dev, 2 * num_chan * chans // LANES, LANES)
    packet_rows = packet[0] * packet[1] * packet[2]
    table = jnp.asarray(fourier_rows(lon_count, lon_pad, mode_dev * devices, mode_dev))
    taken = pl.pallas_call(
        functools.partial(block_kernel, num_lat, num_chan),
        out_shape=jax.ShapeDtypeStruct(packet, bf16),
        in_specs=[smem] * 4 + [hbm] * 5,
        out_specs=hbm,
        scratch_shapes=[
            pltpu.VMEM((lat_dev, chans, lon_count), bf16),
            pltpu.VMEM(disco_weight.shape, bf16),
            pltpu.VMEM(w_up.shape, bf16),
            pltpu.VMEM(w_down.shape, bf16),
            pltpu.VMEM((lat_dev, chans, lon_pad), bf16),
            pltpu.VMEM((chans * HALO * 4 // num_lat, lon_count), bf16),
            pltpu.VMEM((2, HALO, chans, lon_count), bf16),
            pltpu.VMEM((lat_dev + 2 * HALO, chans, lon_pad + LANES), f32),
            pltpu.VMEM((lat_dev, G, S * G), bf16),
            pltpu.VMEM((S * G, CHUNK), bf16),
            pltpu.VMEM((lat_dev, chunks, chans, CHUNK), bf16),
            pltpu.VMEM((chunks, num_chan, chans, CHUNK), bf16),
            pltpu.VMEM((lat_dev, chans * (lon_count % LANES) // LANES, LANES), bf16),
            pltpu.VMEM((num_chan, chans * (lon_count % LANES) // LANES, LANES), bf16),
            pltpu.VMEM((hidden, num_chan * chans), bf16),
            pltpu.VMEM((num_chan * chans, hidden), bf16),
            pltpu.VMEM(table.shape, bf16),
            pltpu.VMEM((2 * mode_dev * devices, num_chan * chans), f32),
            pltpu.VMEM((packet_rows, LANES), f32),
            pltpu.VMEM(packet, bf16),
            dma((6,)),
            dma((2, HALO)),
            dma((2, HALO)),
            dma,
            dma,
            dma,
            dma,
            dma,
            dma((chunks,)),
            dma,
            dma,
            dma,
        ],
        compiler_params=pltpu.CompilerParams(
            collective_id=0, has_side_effects=True, vmem_limit_bytes=56 << 20
        ),
        name="block",
    )(
        support_lat,
        support_lon,
        support_basis,
        support_value,
        jnp.swapaxes(fields, 1, 2),
        disco_weight,
        w_up,
        w_down,
        table,
    )
    return pl.pallas_call(
        legendre_kernel,
        out_shape=jax.ShapeDtypeStruct((mode_dev, degrees, 2 * num_chan * chans), bf16),
        in_specs=[hbm] * 2,
        out_specs=hbm,
        scratch_shapes=[
            pltpu.VMEM(packet, bf16),
            pltpu.VMEM(legendre.shape, bf16),
            pltpu.VMEM((mode_dev, degrees, 2 * num_chan * chans), bf16),
            pltpu.VMEM((packet_rows, LANES), f32),
            dma((2,)),
            dma((mode_dev,)),
        ],
        compiler_params=pltpu.CompilerParams(vmem_limit_bytes=56 << 20),
        name="legendre",
    )(taken, legendre)


def solution(mesh):
    in_specs = (
        P(("tm", "lat"), None, "chan"),
        P(None, "chan", None),
        P("lat", None),
        P("lat", None),
        P("lat", None),
        P("lat", None),
        P(),
        P(),
        P(("lat", "chan"), None, None),
    )
    out_specs = P(("tm", "lat", "chan"), None, None)
    return jax.shard_map(
        on_device, mesh=mesh, in_specs=in_specs, out_specs=out_specs, check_vma=False
    )
```

```python
import functools
import math

import jax
import jax.numpy as jnp
import ml_dtypes
import numpy as np
from jax import lax
from jax.experimental import pallas as pl
from jax.experimental.pallas import tpu as pltpu
from jax.sharding import PartitionSpec as P

G = 64
NB = 6
S = 9
HALO = 2
DLON = 4
LANES = 128
CHUNK = 384
MESH = pl.DeviceIdType.MESH


def fourier_rows(lon_count, lon_pad, mode_count, mode_dev):
    lon = np.arange(lon_count, dtype=np.int64)
    mode = np.arange(mode_count, dtype=np.int64)
    phase = (lon[:, None] * mode[None, :]) % lon_count
    angle = phase.astype(np.float32) * np.float32(2.0 * math.pi / lon_count)
    scale = np.float32(math.sqrt(2.0 / lon_count))
    table = np.zeros((2 * mode_dev, mode_count // mode_dev, lon_pad), np.float32)
    pair = np.stack([np.cos(angle), -np.sin(angle)], axis=-1) * scale
    pair = pair.reshape(lon_count, mode_count // mode_dev, 2 * mode_dev)
    table[:, :, :lon_count] = np.transpose(pair, (2, 1, 0))
    return table.reshape(-1, lon_pad).astype(ml_dtypes.bfloat16)


def spread(block, ext, row, lon_count):
    chans = block.shape[0]
    tiles = -(-lon_count // LANES)
    last = lon_count - (tiles - 1) * LANES
    lane = lax.broadcasted_iota(jnp.int32, (chans, LANES), 1)
    pieces = [block[:, t * LANES : min((t + 1) * LANES, lon_count)].astype(jnp.float32) for t in range(tiles)]
    if last < LANES:
        pieces[-1] = jnp.concatenate([pieces[-1], jnp.zeros((chans, LANES - last), jnp.float32)], axis=1)
    turned = [pltpu.roll(p, DLON, 1) for p in pieces]
    before = pltpu.roll(pieces[-1], (LANES - last + DLON) % LANES, 1)
    after = pltpu.roll(pieces[0], last + DLON, 1)
    for t in range(tiles):
        left = before if t == 0 else turned[t - 1]
        value = jnp.where(lane < DLON, left, turned[t])
        if t == tiles - 1:
            value = jnp.where(lane < last + DLON, value, jnp.where(lane < last + 2 * DLON, after, 0.0))
        ext[row, :, t * LANES : (t + 1) * LANES] = value.astype(ext.dtype)
    ext[row, :, tiles * LANES :] = jnp.zeros((chans, ext.shape[2] - tiles * LANES), ext.dtype)


def make_filters(row, basis, value, weight, filters):
    for pair in range(0, S, 2):
        parts = [
            weight[basis[row, tap]].astype(jnp.float32) * value[row, tap]
            for tap in range(pair, min(pair + 2, S))
        ]
        joined = parts[0] if len(parts) == 1 else jnp.concatenate(parts, axis=1)
        filters[row, :, pair * G : (pair + len(parts)) * G] = joined.astype(filters.dtype)


def disco_chunk(row, start, shift_lat, shift_lon, ext, filters, columns):
    lane = lax.broadcasted_iota(jnp.int32, (G, LANES), 1)
    for tap in range(S):
        source = row + HALO + shift_lat[row, tap]
        turn = DLON + shift_lon[row, tap]
        held = ext[source, :, pl.ds(start, CHUNK + LANES)]
        turned = [
            pltpu.roll(held[:, t * LANES : (t + 1) * LANES], LANES - turn, 1)
            for t in range(CHUNK // LANES + 1)
        ]
        for t in range(CHUNK // LANES):
            columns[tap * G : (tap + 1) * G, t * LANES : (t + 1) * LANES] = jnp.where(
                lane < LANES - turn, turned[t], turned[t + 1]
            ).astype(columns.dtype)
    return jnp.dot(filters[row], columns[...], preferred_element_type=jnp.float32)


def block_kernel(
    num_lat,
    num_chan,
    shift_lat,
    shift_lon,
    basis,
    value,
    fields_hbm,
    weight_hbm,
    up_hbm,
    down_hbm,
    table_hbm,
    taken,
    fields,
    weight,
    w_up,
    w_down,
    own,
    relay,
    halo,
    ext,
    filters,
    columns,
    mixed,
    gathered,
    rest_mixed,
    rest,
    up,
    down,
    table,
    total,
    wide,
    sent,
    load_sem,
    halo_send,
    halo_recv,
    relay_sent,
    relay_recv,
    mix_send,
    last_send,
    rest_send,
    mix_recv,
    rest_recv,
    spec_send,
    spec_recv,
):
    lat_dev, chans, lon_count = fields.shape
    chunks = mixed.shape[1]
    devices = num_lat * num_chan
    half = lat_dev // 2
    per_device = sent.shape[1] * sent.shape[2]
    band = lax.axis_index("lat")
    mine = lax.axis_index("chan")
    me = band * num_chan + mine
    core = lax.rem(band, 2)

    pairs = [
        (fields_hbm, fields),
        (weight_hbm, weight),
        (up_hbm, w_up),
        (down_hbm, w_down),
        (table_hbm, table),
    ]
    loads = [pltpu.make_async_copy(a, b, load_sem.at[i]) for i, (a, b) in enumerate(pairs)]
    for load in loads:
        load.start()
    barrier = pltpu.get_barrier_semaphore()

    def greet(band_to, mine_to):
        pl.semaphore_signal(
            barrier, inc=1, device_id={"lat": band_to, "chan": mine_to}, device_id_type=MESH
        )

    for step in range(1, num_chan):
        greet(band, lax.rem(mine + step, num_chan))

    def greet_band(step, carry):
        for to in range(num_chan):
            greet(lax.rem(band + step, num_lat), to)
        return carry

    lax.fori_loop(1, num_lat, greet_band, 0)
    pl.semaphore_wait(barrier, devices - 1)

    sends = [
        [
            pltpu.make_async_remote_copy(
                src_ref=fields_hbm.at[lat_dev - 1 - step if side == 0 else step],
                dst_ref=halo.at[side, HALO - 1 - step if side == 0 else step],
                send_sem=halo_send.at[side, step],
                recv_sem=halo_recv.at[side, step],
                device_id={"lat": band + 1 if side == 0 else band - 1},
                device_id_type=MESH,
            )
            for step in range(HALO)
        ]
        for side in range(2)
    ]

    seam = num_lat // 2
    ring = seam // 2
    high_z = lax.div(band, seam)
    place = lax.rem(lax.div(band, 2), ring)
    per_lat = ring // HALO
    width = chans // per_lat
    at_seam = jnp.logical_or(band == seam - 1, band == seam)
    is_first = high_z != core

    def part_of(index):
        return lax.div(index, per_lat), pl.ds(pl.multiple_of(lax.rem(index, per_lat) * width, width), width)

    def relay_send(src, sem, to):
        return pltpu.make_async_remote_copy(
            src_ref=src, dst_ref=relay, send_sem=sem, recv_sem=relay_recv,
            device_id={"lat": to}, device_id_type=MESH,
        )

    @pl.when(jnp.logical_and(band < num_lat - 1, band != seam - 1))
    def _():
        for send in sends[0]:
            send.start()

    @pl.when(jnp.logical_and(band > 0, band != seam))
    def _():
        for send in sends[1]:
            send.start()

    for side, source in ((0, seam - 1), (1, seam)):
        @pl.when(band == source)
        def _():
            def start_part(count, carry):
                pace = lax.div(count, 2)
                index = jnp.where(lax.rem(count, 2) == 0, ring // 2 + pace, ring // 2 - 1 - pace)
                index = ring - 1 - index if side == 0 else index
                step, rows = part_of(index)
                to = 2 * index + 1 if side == 0 else seam + 2 * index
                other = source + seam if side == 0 else source - seam
                to = jnp.where(to == source, other, to)
                lat_row = lat_dev - 1 - step if side == 0 else step
                relay_send(fields_hbm.at[lat_row, rows], halo_send.at[side, step], to).start()
                return carry

            lax.fori_loop(0, ring, start_part, 0)

    for load in loads[:2]:
        load.wait()
    for row in range(lat_dev):
        spread(fields[row], ext, HALO + row, lon_count)

    @pl.when(jnp.logical_and(is_first, jnp.logical_not(at_seam)))
    def _():
        pltpu.make_async_copy(relay, relay, relay_recv).wait()
        relay_send(relay, relay_sent, jnp.where(band < seam, band + seam, band - seam)).start()

    left = lon_count % LANES
    whole = lon_count - (chunks - 1) * CHUNK - left
    groups = LANES // left
    tall = chans // groups

    def pack(block):
        return jnp.concatenate(
            [block[g * tall : (g + 1) * tall, whole : whole + left] for g in range(groups)], axis=1
        )

    def unpack(packed):
        value = packed.astype(jnp.float32)
        turned = [value] + [pltpu.roll(value, LANES - g * left, 1) for g in range(1, groups)]
        return jnp.concatenate([t.astype(packed.dtype) for t in turned], axis=0)

    def mix_copy(src, dst, send_sem, recv_sem, to):
        return pltpu.make_async_remote_copy(
            src_ref=src, dst_ref=dst, send_sem=send_sem, recv_sem=recv_sem,
            device_id={"chan": to}, device_id_type=MESH,
        )

    def disco_row(row, to, c):
        start = pl.multiple_of(c * CHUNK, LANES)
        acc = disco_chunk(row, start, shift_lat, shift_lon, ext, filters, columns)
        here = own[row, :, pl.ds(start, CHUNK)].astype(jnp.float32)
        result = (here + acc).astype(mixed.dtype)

        @pl.when(to == mine)
        def _():
            gathered[c, mine] = result

            @pl.when(c == chunks - 1)
            def _():
                rest[mine] = pack(result)

        @pl.when(to != mine)
        def _():
            mixed[to, c] = result

            @pl.when(c < chunks - 1)
            def _():
                mix_copy(mixed.at[to, c], gathered.at[c, mine], mix_send, mix_recv.at[c], to).start()

            @pl.when(c == chunks - 1)
            def _():
                rest_mixed[to] = pack(result)
                src = mixed.at[to, chunks - 1, :, pl.ds(0, whole)]
                dst = gathered.at[chunks - 1, mine, :, pl.ds(0, whole)]
                mix_copy(src, dst, last_send, mix_recv.at[chunks - 1], to).start()
                mix_copy(rest_mixed.at[to], rest.at[mine], rest_send, rest_recv, to).start()

    for row in range(lat_dev):
        own[row, :, :lon_count] = fields[row]
        own[row, :, lon_count:] = jnp.zeros((chans, own.shape[2] - lon_count), own.dtype)
    first = 1 - core
    for turn in range(2):
        side = first if turn == 0 else 1 - first
        present = jnp.where(side == 0, band > 0, band < num_lat - 1)
        for step in range(HALO):
            edge = jnp.where(side == 0, HALO - 1 - step, step)
            row = jnp.where(side == 0, half - 1 - step, half + step)
            make_filters(row, basis, value, weight, filters)
            order = jnp.where(core == 0, step, half - 1 - step)
            to = order * (num_chan - 1) if turn == 0 else order + 1

            @pl.when(present)
            def _():
                arrived = halo.at[side, edge]
                pltpu.make_async_copy(arrived, arrived, halo_recv.at[side, step]).wait()

            @pl.when(jnp.logical_not(present))
            def _():
                halo[side, edge] = jnp.zeros(halo.shape[2:], halo.dtype)

            spread(halo[side, edge], ext, side * (HALO + lat_dev) + edge, lon_count)

            def steps(c, carry):
                disco_row(row, to, c)
                return carry

            lax.fori_loop(0, chunks, steps, 0)
            if turn == 1 and step == 0:

                @pl.when(jnp.logical_not(is_first))
                def _():
                    pltpu.make_async_copy(relay, relay, relay_recv).wait()
                    relay_step, rows = part_of(place)
                    to_side = 1 - core
                    relay_edge = jnp.where(core == 1, HALO - 1 - relay_step, relay_step)
                    pltpu.make_async_remote_copy(
                        src_ref=relay,
                        dst_ref=halo.at[to_side, relay_edge, rows],
                        send_sem=relay_sent,
                        recv_sem=halo_recv.at[to_side, relay_step],
                        device_id={"lat": jnp.where(core == 1, seam, seam - 1)},
                        device_id_type=MESH,
                    ).start()

    for load in loads[2:5]:
        load.wait()
    up[...] = w_up[...].T
    down[...] = w_down[...].T

    def wait_for(ref, sem):
        pltpu.make_async_copy(ref, ref, sem).wait()

    def mlp_part(block, c):
        done = mlp_chunk(block, up[...], down[...])
        wide_lanes = block.shape[1]
        return lax.dot_general(
            table[:, pl.ds(pl.multiple_of(c * CHUNK, LANES), wide_lanes)],
            done,
            (((1,), (1,)), ((), ())),
            preferred_element_type=jnp.float32,
        )

    total[...] = jnp.zeros(total.shape, total.dtype)

    def mlp_step(c, carry):
        wait_for(gathered.at[c, pl.ds(0, num_chan - 1)], mix_recv.at[c])
        total[...] += mlp_part(gathered[c].reshape(num_chan * chans, CHUNK), c)
        return carry

    lax.fori_loop(0, chunks - 1, mlp_step, 0)
    wait_for(gathered.at[chunks - 1, pl.ds(0, num_chan - 1), :, pl.ds(0, whole)], mix_recv.at[chunks - 1])
    wait_for(rest.at[pl.ds(0, num_chan - 1)], rest_recv)
    block = jnp.concatenate([gathered[chunks - 1, p, :, :whole] for p in range(num_chan)], axis=0)
    tail = jnp.concatenate([unpack(rest[p]) for p in range(num_chan)], axis=0)
    total[...] += mlp_part(jnp.concatenate([block, tail], axis=1), chunks - 1)
    for j in range(per_device // 2):
        for h in range(2):
            piece = total[j * devices : (j + 1) * devices, h * LANES : (h + 1) * LANES]
            wide[pl.ds(2 * j + h, devices, stride=per_device), :] = piece
    sent[...] = wide[...].reshape(sent.shape).astype(sent.dtype)

    at_end = jnp.logical_or(mine == 0, mine == num_chan - 1)
    order = jnp.where(at_end, lax.div(mine, num_chan - 1), mine - 1)
    step_here = jnp.where(core == 0, order, half - 1 - order)
    side_here = jnp.where(at_end, first, 1 - first)
    lat = band * lat_dev + jnp.where(side_here == 0, half - 1 - step_here, half + step_here)

    def hand_out(band_to, mine_to):
        pltpu.make_async_remote_copy(
            src_ref=sent.at[band_to * num_chan + mine_to],
            dst_ref=taken.at[lat],
            send_sem=spec_send,
            recv_sem=spec_recv,
            device_id={"lat": band_to, "chan": mine_to},
            device_id_type=MESH,
        ).start()

    def hand_out_band(step, carry):
        for to in range(num_chan):
            hand_out(lax.rem(band + step, num_lat), to)
        return carry

    lax.fori_loop(1, num_lat, hand_out_band, 0)
    for step in range(1, num_chan):
        hand_out(band, lax.rem(mine + step, num_chan))
    keep = pltpu.make_async_copy(sent.at[me], taken.at[lat], load_sem.at[5])
    keep.start()
    keep.wait()
    pltpu.make_async_copy(
        taken.at[pl.ds(0, devices - 1)], taken.at[pl.ds(0, devices - 1)], spec_recv
    ).wait()
    wait_for(mixed.at[pl.ds(0, lat_dev - 1), pl.ds(0, chunks - 1)], mix_send)
    wait_for(mixed.at[pl.ds(0, lat_dev - 1), chunks - 1, :, pl.ds(0, whole)], last_send)
    wait_for(rest_mixed.at[pl.ds(0, lat_dev - 1)], rest_send)
    pltpu.make_async_copy(sent.at[pl.ds(0, devices - 1)], sent.at[pl.ds(0, devices - 1)], spec_send).wait()

    @pl.when(jnp.logical_not(at_seam))
    def _():
        pltpu.make_async_copy(relay, relay, relay_sent).wait()

    @pl.when(band < num_lat - 1)
    def _():
        for send in sends[0]:
            send.wait_send()

    @pl.when(band > 0)
    def _():
        for send in sends[1]:
            send.wait_send()


def mlp_chunk(mixed, up, down):
    values = mixed.astype(jnp.float32)
    center = values - jnp.mean(values, axis=0, keepdims=True)
    variance = jnp.mean(center * center, axis=0, keepdims=True)
    normed = (center * lax.rsqrt(variance + 1e-05)).astype(jnp.bfloat16)
    lifted = jnp.dot(up, normed, preferred_element_type=jnp.float32)
    inner = math.sqrt(2.0 / math.pi) * (lifted + 0.044715 * (lifted * lifted * lifted))
    active = (0.5 * lifted * (1.0 + jnp.tanh(inner))).astype(jnp.bfloat16)
    lowered = jnp.dot(down, active, preferred_element_type=jnp.float32)
    return (values + lowered).astype(jnp.bfloat16)


def legendre_kernel(taken_hbm, legendre_hbm, out_hbm, taken, legendre, out, wide, load_sem, out_sem):
    mode_dev, degrees, lats = legendre.shape
    loads = [
        pltpu.make_async_copy(legendre_hbm, legendre, load_sem.at[0]),
        pltpu.make_async_copy(taken_hbm, taken, load_sem.at[1]),
    ]
    for load in loads:
        load.start()
    me = lax.axis_index("lat") * lax.axis_size("chan") + lax.axis_index("chan")
    degree = lax.broadcasted_iota(jnp.int32, (degrees, lats), 0)
    loads[0].wait()
    for m in range(mode_dev):
        kept = jnp.where(degree >= me * mode_dev + m, legendre[m].astype(jnp.float32), 0.0)
        legendre[m] = kept.astype(jnp.bfloat16)
    loads[1].wait()
    wide[...] = taken[...].astype(jnp.float32).reshape(wide.shape)
    each = wide.shape[0] // lats
    per_mode = each // mode_dev
    stores = [pltpu.make_async_copy(out.at[m], out_hbm.at[m], out_sem.at[m]) for m in range(mode_dev)]
    for m in range(mode_dev):
        right = jnp.concatenate(
            [
                wide[pl.ds(m * per_mode + j, lats, stride=each), :].astype(jnp.bfloat16)
                for j in range(per_mode)
            ],
            axis=1,
        )
        out[m] = jnp.dot(legendre[m], right, preferred_element_type=jnp.float32).astype(out.dtype)
        stores[m].start()
    for store in stores:
        store.wait()


def on_device(
    fields, disco_weight, support_lat, support_lon, support_basis, support_value, w_up, w_down, legendre
):
    lat_dev, lon_count, chans = fields.shape
    num_lat = lax.axis_size("lat")
    num_chan = lax.axis_size("chan")
    mode_dev, degrees, lats = legendre.shape
    devices = num_lat * num_chan
    chunks = -(-lon_count // CHUNK)
    lon_pad = chunks * CHUNK
    hidden = w_up.shape[1]
    smem = pl.BlockSpec(memory_space=pltpu.SMEM)
    hbm = pl.BlockSpec(memory_space=pltpu.HBM)
    bf16, f32 = jnp.bfloat16, jnp.float32
    dma = pltpu.SemaphoreType.DMA
    packet = (devices, mode_dev, 2 * num_chan * chans // LANES, LANES)
    packet_rows = packet[0] * packet[1] * packet[2]
    table = jnp.asarray(fourier_rows(lon_count, lon_pad, mode_dev * devices, mode_dev))
    taken = pl.pallas_call(
        functools.partial(block_kernel, num_lat, num_chan),
        out_shape=jax.ShapeDtypeStruct(packet, bf16),
        in_specs=[smem] * 4 + [hbm] * 5,
        out_specs=hbm,
        scratch_shapes=[
            pltpu.VMEM((lat_dev, chans, lon_count), bf16),
            pltpu.VMEM(disco_weight.shape, bf16),
            pltpu.VMEM(w_up.shape, bf16),
            pltpu.VMEM(w_down.shape, bf16),
            pltpu.VMEM((lat_dev, chans, lon_pad), bf16),
            pltpu.VMEM((chans * HALO * 4 // num_lat, lon_count), bf16),
            pltpu.VMEM((2, HALO, chans, lon_count), bf16),
            pltpu.VMEM((lat_dev + 2 * HALO, chans, lon_pad + LANES), f32),
            pltpu.VMEM((lat_dev, G, S * G), bf16),
            pltpu.VMEM((S * G, CHUNK), bf16),
            pltpu.VMEM((lat_dev, chunks, chans, CHUNK), bf16),
            pltpu.VMEM((chunks, num_chan, chans, CHUNK), bf16),
            pltpu.VMEM((lat_dev, chans * (lon_count % LANES) // LANES, LANES), bf16),
            pltpu.VMEM((num_chan, chans * (lon_count % LANES) // LANES, LANES), bf16),
            pltpu.VMEM((hidden, num_chan * chans), bf16),
            pltpu.VMEM((num_chan * chans, hidden), bf16),
            pltpu.VMEM(table.shape, bf16),
            pltpu.VMEM((2 * mode_dev * devices, num_chan * chans), f32),
            pltpu.VMEM((packet_rows, LANES), f32),
            pltpu.VMEM(packet, bf16),
            dma((6,)),
            dma((2, HALO)),
            dma((2, HALO)),
            dma,
            dma,
            dma,
            dma,
            dma,
            dma((chunks,)),
            dma,
            dma,
            dma,
        ],
        compiler_params=pltpu.CompilerParams(
            collective_id=0, has_side_effects=True, vmem_limit_bytes=56 << 20
        ),
        name="block",
    )(
        support_lat,
        support_lon,
        support_basis,
        support_value,
        jnp.swapaxes(fields, 1, 2),
        disco_weight,
        w_up,
        w_down,
        table,
    )
    return pl.pallas_call(
        legendre_kernel,
        out_shape=jax.ShapeDtypeStruct((mode_dev, degrees, 2 * num_chan * chans), bf16),
        in_specs=[hbm] * 2,
        out_specs=hbm,
        scratch_shapes=[
            pltpu.VMEM(packet, bf16),
            pltpu.VMEM(legendre.shape, bf16),
            pltpu.VMEM((mode_dev, degrees, 2 * num_chan * chans), bf16),
            pltpu.VMEM((packet_rows, LANES), f32),
            dma((2,)),
            dma((mode_dev,)),
        ],
        compiler_params=pltpu.CompilerParams(vmem_limit_bytes=56 << 20),
        name="legendre",
    )(taken, legendre)


def solution(mesh):
    in_specs = (
        P(("tm", "lat"), None, "chan"),
        P(None, "chan", None),
        P("lat", None),
        P("lat", None),
        P("lat", None),
        P("lat", None),
        P(),
        P(),
        P(("lat", "chan"), None, None),
    )
    out_specs = P(("tm", "lat", "chan"), None, None)
    return jax.shard_map(
        on_device, mesh=mesh, in_specs=in_specs, out_specs=out_specs, check_vma=False
    )
```

```python
import functools
import math

import jax
import jax.numpy as jnp
import ml_dtypes
import numpy as np
from jax import lax
from jax.experimental import pallas as pl
from jax.experimental.pallas import tpu as pltpu
from jax.sharding import PartitionSpec as P

G = 64
NB = 6
S = 9
HALO = 2
DLON = 4
LANES = 128
CHUNK = 384
MESH = pl.DeviceIdType.MESH


def fourier_rows(lon_count, lon_pad, mode_count, mode_dev):
    lon = np.arange(lon_count, dtype=np.int64)
    mode = np.arange(mode_count, dtype=np.int64)
    phase = (lon[:, None] * mode[None, :]) % lon_count
    angle = phase.astype(np.float32) * np.float32(2.0 * math.pi / lon_count)
    scale = np.float32(math.sqrt(2.0 / lon_count))
    table = np.zeros((2 * mode_dev, mode_count // mode_dev, lon_pad), np.float32)
    pair = np.stack([np.cos(angle), -np.sin(angle)], axis=-1) * scale
    pair = pair.reshape(lon_count, mode_count // mode_dev, 2 * mode_dev)
    table[:, :, :lon_count] = np.transpose(pair, (2, 1, 0))
    return table.reshape(-1, lon_pad).astype(ml_dtypes.bfloat16)


def spread(block, ext, row, lon_count):
    chans = block.shape[0]
    tiles = -(-lon_count // LANES)
    last = lon_count - (tiles - 1) * LANES
    lane = lax.broadcasted_iota(jnp.int32, (chans, LANES), 1)
    pieces = [block[:, t * LANES : min((t + 1) * LANES, lon_count)].astype(jnp.float32) for t in range(tiles)]
    if last < LANES:
        pieces[-1] = jnp.concatenate([pieces[-1], jnp.zeros((chans, LANES - last), jnp.float32)], axis=1)
    turned = [pltpu.roll(p, DLON, 1) for p in pieces]
    before = pltpu.roll(pieces[-1], (LANES - last + DLON) % LANES, 1)
    after = pltpu.roll(pieces[0], last + DLON, 1)
    for t in range(tiles):
        left = before if t == 0 else turned[t - 1]
        value = jnp.where(lane < DLON, left, turned[t])
        if t == tiles - 1:
            value = jnp.where(lane < last + DLON, value, jnp.where(lane < last + 2 * DLON, after, 0.0))
        ext[row, :, t * LANES : (t + 1) * LANES] = value.astype(ext.dtype)
    ext[row, :, tiles * LANES :] = jnp.zeros((chans, ext.shape[2] - tiles * LANES), ext.dtype)


def make_filters(row, basis, value, weight, filters):
    for pair in range(0, S, 2):
        parts = [
            weight[basis[row, tap]].astype(jnp.float32) * value[row, tap]
            for tap in range(pair, min(pair + 2, S))
        ]
        joined = parts[0] if len(parts) == 1 else jnp.concatenate(parts, axis=1)
        filters[row, :, pair * G : (pair + len(parts)) * G] = joined.astype(filters.dtype)


def disco_chunk(row, start, shift_lat, shift_lon, ext, filters, columns):
    lane = lax.broadcasted_iota(jnp.int32, (G, LANES), 1)
    for tap in range(S):
        source = row + HALO + shift_lat[row, tap]
        turn = DLON + shift_lon[row, tap]
        held = ext[source, :, pl.ds(start, CHUNK + LANES)]
        turned = [
            pltpu.roll(held[:, t * LANES : (t + 1) * LANES], LANES - turn, 1)
            for t in range(CHUNK // LANES + 1)
        ]
        for t in range(CHUNK // LANES):
            columns[tap * G : (tap + 1) * G, t * LANES : (t + 1) * LANES] = jnp.where(
                lane < LANES - turn, turned[t], turned[t + 1]
            ).astype(columns.dtype)
    return jnp.dot(filters[row], columns[...], preferred_element_type=jnp.float32)


def block_kernel(
    num_lat,
    num_chan,
    shift_lat,
    shift_lon,
    basis,
    value,
    fields_hbm,
    weight_hbm,
    up_hbm,
    down_hbm,
    table_hbm,
    taken,
    fields,
    weight,
    w_up,
    w_down,
    own,
    relay,
    halo,
    ext,
    filters,
    columns,
    mixed,
    gathered,
    rest_mixed,
    rest,
    up,
    down,
    table,
    total,
    wide,
    sent,
    load_sem,
    halo_send,
    halo_recv,
    relay_sent,
    relay_recv,
    mix_send,
    last_send,
    rest_send,
    mix_recv,
    rest_recv,
    spec_send,
    spec_recv,
):
    lat_dev, chans, lon_count = fields.shape
    chunks = mixed.shape[1]
    devices = num_lat * num_chan
    half = lat_dev // 2
    per_device = sent.shape[1] * sent.shape[2]
    band = lax.axis_index("lat")
    mine = lax.axis_index("chan")
    me = band * num_chan + mine
    core = lax.rem(band, 2)

    pairs = [
        (fields_hbm, fields),
        (weight_hbm, weight),
        (up_hbm, w_up),
        (down_hbm, w_down),
        (table_hbm, table),
    ]
    loads = [pltpu.make_async_copy(a, b, load_sem.at[i]) for i, (a, b) in enumerate(pairs)]
    for load in loads:
        load.start()
    barrier = pltpu.get_barrier_semaphore()

    def greet(band_to, mine_to):
        pl.semaphore_signal(
            barrier, inc=1, device_id={"lat": band_to, "chan": mine_to}, device_id_type=MESH
        )

    for step in range(1, num_chan):
        greet(band, lax.rem(mine + step, num_chan))

    def greet_band(step, carry):
        for to in range(num_chan):
            greet(lax.rem(band + step, num_lat), to)
        return carry

    lax.fori_loop(1, num_lat, greet_band, 0)
    pl.semaphore_wait(barrier, devices - 1)

    sends = [
        [
            pltpu.make_async_remote_copy(
                src_ref=fields_hbm.at[lat_dev - 1 - step if side == 0 else step],
                dst_ref=halo.at[side, HALO - 1 - step if side == 0 else step],
                send_sem=halo_send.at[side, step],
                recv_sem=halo_recv.at[side, step],
                device_id={"lat": band + 1 if side == 0 else band - 1},
                device_id_type=MESH,
            )
            for step in range(HALO)
        ]
        for side in range(2)
    ]

    seam = num_lat // 2
    ring = seam // 2
    high_z = lax.div(band, seam)
    place = lax.rem(lax.div(band, 2), ring)
    per_lat = ring // HALO
    width = chans // per_lat
    at_seam = jnp.logical_or(band == seam - 1, band == seam)
    is_first = high_z != core

    def part_of(index):
        return lax.div(index, per_lat), pl.ds(pl.multiple_of(lax.rem(index, per_lat) * width, width), width)

    def relay_send(src, sem, to):
        return pltpu.make_async_remote_copy(
            src_ref=src, dst_ref=relay, send_sem=sem, recv_sem=relay_recv,
            device_id={"lat": to}, device_id_type=MESH,
        )

    @pl.when(jnp.logical_and(band < num_lat - 1, band != seam - 1))
    def _():
        for send in sends[0]:
            send.start()

    @pl.when(jnp.logical_and(band > 0, band != seam))
    def _():
        for send in sends[1]:
            send.start()

    for side, source in ((0, seam - 1), (1, seam)):
        @pl.when(band == source)
        def _():
            def start_part(count, carry):
                pace = lax.div(count, 2)
                index = jnp.where(lax.rem(count, 2) == 0, ring // 2 + pace, ring // 2 - 1 - pace)
                index = ring - 1 - index if side == 0 else index
                step, rows = part_of(index)
                to = 2 * index + 1 if side == 0 else seam + 2 * index
                other = source + seam if side == 0 else source - seam
                to = jnp.where(to == source, other, to)
                lat_row = lat_dev - 1 - step if side == 0 else step
                relay_send(fields_hbm.at[lat_row, rows], halo_send.at[side, step], to).start()
                return carry

            lax.fori_loop(0, ring, start_part, 0)

    for load in loads[:2]:
        load.wait()
    for row in range(lat_dev):
        spread(fields[row], ext, HALO + row, lon_count)

    @pl.when(jnp.logical_and(is_first, jnp.logical_not(at_seam)))
    def _():
        pltpu.make_async_copy(relay, relay, relay_recv).wait()
        relay_send(relay, relay_sent, jnp.where(band < seam, band + seam, band - seam)).start()

    left = lon_count % LANES
    whole = lon_count - (chunks - 1) * CHUNK - left
    groups = LANES // left
    tall = chans // groups

    def pack(block):
        return jnp.concatenate(
            [block[g * tall : (g + 1) * tall, whole : whole + left] for g in range(groups)], axis=1
        )

    def unpack(packed):
        value = packed.astype(jnp.float32)
        turned = [value] + [pltpu.roll(value, LANES - g * left, 1) for g in range(1, groups)]
        return jnp.concatenate([t.astype(packed.dtype) for t in turned], axis=0)

    def mix_copy(src, dst, send_sem, recv_sem, to):
        return pltpu.make_async_remote_copy(
            src_ref=src, dst_ref=dst, send_sem=send_sem, recv_sem=recv_sem,
            device_id={"chan": to}, device_id_type=MESH,
        )

    def disco_row(row, to, c):
        start = pl.multiple_of(c * CHUNK, LANES)
        acc = disco_chunk(row, start, shift_lat, shift_lon, ext, filters, columns)
        here = own[row, :, pl.ds(start, CHUNK)].astype(jnp.float32)
        result = (here + acc).astype(mixed.dtype)

        @pl.when(to == mine)
        def _():
            gathered[c, mine] = result

            @pl.when(c == chunks - 1)
            def _():
                rest[mine] = pack(result)

        @pl.when(to != mine)
        def _():
            mixed[to, c] = result

            @pl.when(c < chunks - 1)
            def _():
                mix_copy(mixed.at[to, c], gathered.at[c, mine], mix_send, mix_recv.at[c], to).start()

            @pl.when(c == chunks - 1)
            def _():
                rest_mixed[to] = pack(result)
                src = mixed.at[to, chunks - 1, :, pl.ds(0, whole)]
                dst = gathered.at[chunks - 1, mine, :, pl.ds(0, whole)]
                mix_copy(src, dst, last_send, mix_recv.at[chunks - 1], to).start()
                mix_copy(rest_mixed.at[to], rest.at[mine], rest_send, rest_recv, to).start()

    for row in range(lat_dev):
        own[row, :, :lon_count] = fields[row]
        own[row, :, lon_count:] = jnp.zeros((chans, own.shape[2] - lon_count), own.dtype)
    first = 1 - core
    for turn in range(2):
        side = first if turn == 0 else 1 - first
        present = jnp.where(side == 0, band > 0, band < num_lat - 1)
        for step in range(HALO):
            edge = jnp.where(side == 0, HALO - 1 - step, step)
            row = jnp.where(side == 0, half - 1 - step, half + step)
            make_filters(row, basis, value, weight, filters)
            order = jnp.where(core == 0, step, half - 1 - step)
            to = order * (num_chan - 1) if turn == 0 else order + 1

            @pl.when(present)
            def _():
                arrived = halo.at[side, edge]
                pltpu.make_async_copy(arrived, arrived, halo_recv.at[side, step]).wait()

            @pl.when(jnp.logical_not(present))
            def _():
                halo[side, edge] = jnp.zeros(halo.shape[2:], halo.dtype)

            spread(halo[side, edge], ext, side * (HALO + lat_dev) + edge, lon_count)

            def steps(c, carry):
                disco_row(row, to, c)
                return carry

            lax.fori_loop(0, chunks, steps, 0)
            if turn == 1 and step == 0:

                @pl.when(jnp.logical_not(is_first))
                def _():
                    pltpu.make_async_copy(relay, relay, relay_recv).wait()
                    relay_step, rows = part_of(place)
                    to_side = 1 - core
                    relay_edge = jnp.where(core == 1, HALO - 1 - relay_step, relay_step)
                    pltpu.make_async_remote_copy(
                        src_ref=relay,
                        dst_ref=halo.at[to_side, relay_edge, rows],
                        send_sem=relay_sent,
                        recv_sem=halo_recv.at[to_side, relay_step],
                        device_id={"lat": jnp.where(core == 1, seam, seam - 1)},
                        device_id_type=MESH,
                    ).start()

    for load in loads[2:5]:
        load.wait()
    up[...] = w_up[...].T
    down[...] = w_down[...].T

    def wait_for(ref, sem):
        pltpu.make_async_copy(ref, ref, sem).wait()

    def mlp_part(block, c):
        done = mlp_chunk(block, up[...], down[...])
        wide_lanes = block.shape[1]
        return lax.dot_general(
            table[:, pl.ds(pl.multiple_of(c * CHUNK, LANES), wide_lanes)],
            done,
            (((1,), (1,)), ((), ())),
            preferred_element_type=jnp.float32,
        )

    total[...] = jnp.zeros(total.shape, total.dtype)

    def mlp_step(c, carry):
        wait_for(gathered.at[c, pl.ds(0, num_chan - 1)], mix_recv.at[c])
        total[...] += mlp_part(gathered[c].reshape(num_chan * chans, CHUNK), c)
        return carry

    lax.fori_loop(0, chunks - 1, mlp_step, 0)
    wait_for(gathered.at[chunks - 1, pl.ds(0, num_chan - 1), :, pl.ds(0, whole)], mix_recv.at[chunks - 1])
    wait_for(rest.at[pl.ds(0, num_chan - 1)], rest_recv)
    block = jnp.concatenate([gathered[chunks - 1, p, :, :whole] for p in range(num_chan)], axis=0)
    tail = jnp.concatenate([unpack(rest[p]) for p in range(num_chan)], axis=0)
    total[...] += mlp_part(jnp.concatenate([block, tail], axis=1), chunks - 1)
    for j in range(per_device // 2):
        for h in range(2):
            piece = total[j * devices : (j + 1) * devices, h * LANES : (h + 1) * LANES]
            wide[pl.ds(2 * j + h, devices, stride=per_device), :] = piece
    sent[...] = wide[...].reshape(sent.shape).astype(sent.dtype)

    at_end = jnp.logical_or(mine == 0, mine == num_chan - 1)
    order = jnp.where(at_end, lax.div(mine, num_chan - 1), mine - 1)
    step_here = jnp.where(core == 0, order, half - 1 - order)
    side_here = jnp.where(at_end, first, 1 - first)
    lat = band * lat_dev + jnp.where(side_here == 0, half - 1 - step_here, half + step_here)

    def hand_out(band_to, mine_to):
        pltpu.make_async_remote_copy(
            src_ref=sent.at[band_to * num_chan + mine_to],
            dst_ref=taken.at[lat],
            send_sem=spec_send,
            recv_sem=spec_recv,
            device_id={"lat": band_to, "chan": mine_to},
            device_id_type=MESH,
        ).start()

    def hand_out_band(step, carry):
        for turn in range(num_chan):
            hand_out(lax.rem(band + step, num_lat), lax.rem(mine + turn, num_chan))
        return carry

    lax.fori_loop(1, num_lat, hand_out_band, 0)
    for step in range(1, num_chan):
        hand_out(band, lax.rem(mine + step, num_chan))
    keep = pltpu.make_async_copy(sent.at[me], taken.at[lat], load_sem.at[5])
    keep.start()
    keep.wait()
    pltpu.make_async_copy(
        taken.at[pl.ds(0, devices - 1)], taken.at[pl.ds(0, devices - 1)], spec_recv
    ).wait()
    wait_for(mixed.at[pl.ds(0, lat_dev - 1), pl.ds(0, chunks - 1)], mix_send)
    wait_for(mixed.at[pl.ds(0, lat_dev - 1), chunks - 1, :, pl.ds(0, whole)], last_send)
    wait_for(rest_mixed.at[pl.ds(0, lat_dev - 1)], rest_send)
    pltpu.make_async_copy(sent.at[pl.ds(0, devices - 1)], sent.at[pl.ds(0, devices - 1)], spec_send).wait()

    @pl.when(jnp.logical_not(at_seam))
    def _():
        pltpu.make_async_copy(relay, relay, relay_sent).wait()

    @pl.when(band < num_lat - 1)
    def _():
        for send in sends[0]:
            send.wait_send()

    @pl.when(band > 0)
    def _():
        for send in sends[1]:
            send.wait_send()


def mlp_chunk(mixed, up, down):
    values = mixed.astype(jnp.float32)
    center = values - jnp.mean(values, axis=0, keepdims=True)
    variance = jnp.mean(center * center, axis=0, keepdims=True)
    normed = (center * lax.rsqrt(variance + 1e-05)).astype(jnp.bfloat16)
    lifted = jnp.dot(up, normed, preferred_element_type=jnp.float32)
    inner = math.sqrt(2.0 / math.pi) * (lifted + 0.044715 * (lifted * lifted * lifted))
    active = (0.5 * lifted * (1.0 + jnp.tanh(inner))).astype(jnp.bfloat16)
    lowered = jnp.dot(down, active, preferred_element_type=jnp.float32)
    return (values + lowered).astype(jnp.bfloat16)


def legendre_kernel(taken_hbm, legendre_hbm, out_hbm, taken, legendre, out, wide, load_sem, out_sem):
    mode_dev, degrees, lats = legendre.shape
    loads = [
        pltpu.make_async_copy(legendre_hbm, legendre, load_sem.at[0]),
        pltpu.make_async_copy(taken_hbm, taken, load_sem.at[1]),
    ]
    for load in loads:
        load.start()
    me = lax.axis_index("lat") * lax.axis_size("chan") + lax.axis_index("chan")
    degree = lax.broadcasted_iota(jnp.int32, (degrees, lats), 0)
    loads[0].wait()
    for m in range(mode_dev):
        kept = jnp.where(degree >= me * mode_dev + m, legendre[m].astype(jnp.float32), 0.0)
        legendre[m] = kept.astype(jnp.bfloat16)
    loads[1].wait()
    wide[...] = taken[...].astype(jnp.float32).reshape(wide.shape)
    each = wide.shape[0] // lats
    per_mode = each // mode_dev
    stores = [pltpu.make_async_copy(out.at[m], out_hbm.at[m], out_sem.at[m]) for m in range(mode_dev)]
    for m in range(mode_dev):
        right = jnp.concatenate(
            [
                wide[pl.ds(m * per_mode + j, lats, stride=each), :].astype(jnp.bfloat16)
                for j in range(per_mode)
            ],
            axis=1,
        )
        out[m] = jnp.dot(legendre[m], right, preferred_element_type=jnp.float32).astype(out.dtype)
        stores[m].start()
    for store in stores:
        store.wait()


def on_device(
    fields, disco_weight, support_lat, support_lon, support_basis, support_value, w_up, w_down, legendre
):
    lat_dev, lon_count, chans = fields.shape
    num_lat = lax.axis_size("lat")
    num_chan = lax.axis_size("chan")
    mode_dev, degrees, lats = legendre.shape
    devices = num_lat * num_chan
    chunks = -(-lon_count // CHUNK)
    lon_pad = chunks * CHUNK
    hidden = w_up.shape[1]
    smem = pl.BlockSpec(memory_space=pltpu.SMEM)
    hbm = pl.BlockSpec(memory_space=pltpu.HBM)
    bf16, f32 = jnp.bfloat16, jnp.float32
    dma = pltpu.SemaphoreType.DMA
    packet = (devices, mode_dev, 2 * num_chan * chans // LANES, LANES)
    packet_rows = packet[0] * packet[1] * packet[2]
    table = jnp.asarray(fourier_rows(lon_count, lon_pad, mode_dev * devices, mode_dev))
    taken = pl.pallas_call(
        functools.partial(block_kernel, num_lat, num_chan),
        out_shape=jax.ShapeDtypeStruct(packet, bf16),
        in_specs=[smem] * 4 + [hbm] * 5,
        out_specs=hbm,
        scratch_shapes=[
            pltpu.VMEM((lat_dev, chans, lon_count), bf16),
            pltpu.VMEM(disco_weight.shape, bf16),
            pltpu.VMEM(w_up.shape, bf16),
            pltpu.VMEM(w_down.shape, bf16),
            pltpu.VMEM((lat_dev, chans, lon_pad), bf16),
            pltpu.VMEM((chans * HALO * 4 // num_lat, lon_count), bf16),
            pltpu.VMEM((2, HALO, chans, lon_count), bf16),
            pltpu.VMEM((lat_dev + 2 * HALO, chans, lon_pad + LANES), f32),
            pltpu.VMEM((lat_dev, G, S * G), bf16),
            pltpu.VMEM((S * G, CHUNK), bf16),
            pltpu.VMEM((lat_dev, chunks, chans, CHUNK), bf16),
            pltpu.VMEM((chunks, num_chan, chans, CHUNK), bf16),
            pltpu.VMEM((lat_dev, chans * (lon_count % LANES) // LANES, LANES), bf16),
            pltpu.VMEM((num_chan, chans * (lon_count % LANES) // LANES, LANES), bf16),
            pltpu.VMEM((hidden, num_chan * chans), bf16),
            pltpu.VMEM((num_chan * chans, hidden), bf16),
            pltpu.VMEM(table.shape, bf16),
            pltpu.VMEM((2 * mode_dev * devices, num_chan * chans), f32),
            pltpu.VMEM((packet_rows, LANES), f32),
            pltpu.VMEM(packet, bf16),
            dma((6,)),
            dma((2, HALO)),
            dma((2, HALO)),
            dma,
            dma,
            dma,
            dma,
            dma,
            dma((chunks,)),
            dma,
            dma,
            dma,
        ],
        compiler_params=pltpu.CompilerParams(
            collective_id=0, has_side_effects=True, vmem_limit_bytes=56 << 20
        ),
        name="block",
    )(
        support_lat,
        support_lon,
        support_basis,
        support_value,
        jnp.swapaxes(fields, 1, 2),
        disco_weight,
        w_up,
        w_down,
        table,
    )
    return pl.pallas_call(
        legendre_kernel,
        out_shape=jax.ShapeDtypeStruct((mode_dev, degrees, 2 * num_chan * chans), bf16),
        in_specs=[hbm] * 2,
        out_specs=hbm,
        scratch_shapes=[
            pltpu.VMEM(packet, bf16),
            pltpu.VMEM(legendre.shape, bf16),
            pltpu.VMEM((mode_dev, degrees, 2 * num_chan * chans), bf16),
            pltpu.VMEM((packet_rows, LANES), f32),
            dma((2,)),
            dma((mode_dev,)),
        ],
        compiler_params=pltpu.CompilerParams(vmem_limit_bytes=56 << 20),
        name="legendre",
    )(taken, legendre)


def solution(mesh):
    in_specs = (
        P(("tm", "lat"), None, "chan"),
        P(None, "chan", None),
        P("lat", None),
        P("lat", None),
        P("lat", None),
        P("lat", None),
        P(),
        P(),
        P(("lat", "chan"), None, None),
    )
    out_specs = P(("tm", "lat", "chan"), None, None)
    return jax.shard_map(
        on_device, mesh=mesh, in_specs=in_specs, out_specs=out_specs, check_vma=False
    )
```
